256 devices in a mesh: ctx: 16 (over z_lo, y, core), tp: 16 (over x, z_hi).
Axes of the slice: x: 4, y: 4, z: 8 (z_hi: 4, z_lo: 2; z = z_hi * 2 + z_lo), core: 2. Of those that a mesh axis runs over, the one named last changes fastest.
Arguments:
- tokens: bfloat16 [4096, 4096], P('ctx', 'tp'), may hold values from -6 to 6
- cotangent: bfloat16 [4096, 4096], P('ctx', 'tp'), may hold values from -6 to 6
- norm_gain: bfloat16 [4096], P('tp'), may hold values from 0.25 to 1.75
- in_weight: bfloat16 [4096, 3, 4096], P(None, None, 'tp'), may hold values from -0.09375 to 0.09375
- in_down: bfloat16 [4096, 256], P('tp'), may hold values from -0.09375 to 0.09375
- in_up: bfloat16 [256, 3, 4096], P(None, None, 'tp'), may hold values from -0.375 to 0.375
- in_scale: float32 [3, 4096], P(None, 'tp'), may hold values from -3 to 3
- scale_table: float32 [4, 256], replicated, may hold values from -4 to 4
- table_pick: int32 [4], replicated, may hold values from 0 to 3
- short_taps: float32 [3, 3, 4096], P(None, None, 'tp'), may hold values from -3.5 to 3.5
- residue: float32 [4096], P('tp'), may hold values from -3 to 3
- decay: float32 [4096], P('tp'), may hold values from 1.2207031e-05 to 0.0333333333
- skip_gain: float32 [4096], P('tp'), may hold values from 0.5 to 1.5
- out_weight: bfloat16 [4096, 4096], P('tp'), may hold values from -0.09375 to 0.09375
- out_down: bfloat16 [4096, 256], P('tp'), may hold values from -0.09375 to 0.09375
- out_up: bfloat16 [256, 4096], P(None, 'tp'), may hold values from -0.375 to 0.375
- out_scale: float32 [4096], P('tp'), may hold values from -3 to 3
Outputs:
- mixed: bfloat16 [4096, 4096], P('ctx', 'tp')
- grad_tokens: bfloat16 [4096, 4096], P('ctx', 'tp')
- grad_table: float32 [4, 256], replicated
- grad_in_scale: float32 [3, 4096], P(None, 'tp')
- grad_out_scale: float32 [4096], P('tp')
The draws below stay inside these ranges and needn't reach their ends.
All inputs are finite; a program needn't handle non-finite values.
Results may differ from the reference program's by a relative error of at most 0.039.
Values may be sent and summed in bfloat16 or wider, within the bound.
No kernel may reach another device: no remote copies, remote signals or barrier semaphores. Data moves between devices by JAX's collectives and lax.ppermute only.
A program may use at most 64 MiB of HBM per device.

```python
import math
import jax
import jax.numpy as jnp
from jax import lax

D = 4096
TAPS = 3
R = 256
G = 4
L = 4096
N_TP = 16


def draw_decay(key, part):
    key = jax.random.fold_in(key, 5)
    lower = math.log(0.2 / L)
    upper = math.log(1.0 / 30.0)
    return jnp.exp(jax.random.uniform(key, (D,), jnp.float32, lower, upper))


def with_ends(drawn, stream_key, least, high):
    longest = drawn.shape.index(max(drawn.shape))
    spots = []
    for shift in (0, 1):
        where = [jax.random.randint(jax.random.fold_in(stream_key, axis), (), 0, length) for axis, length in enumerate(drawn.shape)]
        where[longest] = (where[longest] + shift) % drawn.shape[longest]
        spots.append(tuple(where))
    return drawn.at[spots[0]].set(least).at[spots[1]].set(high)


def block_scale(own_key, dims, shards, least, largest):
    factor_of = 1.0
    for dim, blocks in shards:
        heights = jax.random.uniform(jax.random.fold_in(jax.random.fold_in(own_key, 6), dim), (blocks,), jnp.float32, least / len(shards), largest / len(shards))
        factor_of = factor_of * jnp.repeat(jnp.exp(heights), dims[dim] // blocks).reshape((-1,) + (1,) * (len(dims) - 1 - dim))
    return factor_of


def gaussian(key, dims, spread, most, cuts=(), held_as=jnp.bfloat16):
    entries = spread * jax.random.normal(key, dims, jnp.float32)
    if cuts:
        entries = entries * block_scale(key, dims, cuts, -0.22, 0.18)
    return jnp.clip(entries, -most, most).astype(held_as)


def setup_inputs(seed: int = 0) -> dict:
    splits = jax.random.split(jax.random.key(seed), 18)
    tokens = gaussian(splits[0], (L, D), 1.0, 6.0, ((0, 16), (1, 16)))
    cotangent = gaussian(splits[1], (L, D), 1.0, 6.0, ((0, 16), (1, 16)))
    norm_gain = jnp.clip(1.0 + 0.15 * jax.random.normal(splits[2], (D,), jnp.float32), 0.25, 1.75).astype(jnp.bfloat16)
    in_weight = gaussian(splits[3], (D, 3, D), D ** -0.5, 0.09375, ((2, 16),))
    in_down = gaussian(splits[4], (D, R), D ** -0.5, 0.09375, ((0, 16),))
    in_up = gaussian(splits[5], (R, 3, D), R ** -0.5, 0.375, ((2, 16),))
    in_scale = gaussian(splits[6], (3, D), 0.5, 3.0, ((1, 16),), jnp.float32)
    scale_table = gaussian(splits[7], (G, R), 1.0, 4.0, (), jnp.float32)
    table_pick = with_ends(jax.random.randint(splits[8], (4,), 0, G), jax.random.fold_in(splits[8], 1), 0, G - 1).astype(jnp.int32)
    short_taps = gaussian(splits[9], (3, TAPS, D), TAPS ** -0.5, 3.5, ((2, 16),), jnp.float32)
    residue = gaussian(splits[10], (D,), 1.0, 3.0, ((0, 16),), jnp.float32)
    decay = draw_decay(jax.random.fold_in(splits[17], 71), 0)
    skip_gain = jnp.clip(0.5 + 1.0 * jax.random.uniform(splits[12], (D,), jnp.float32) ** block_scale(splits[12], (D,), ((0, 16),), -0.2, 0.2), 0.5, 1.5)
    out_weight = gaussian(splits[13], (D, D), D ** -0.5, 0.09375, ((0, 16),))
    out_down = gaussian(splits[14], (D, R), D ** -0.5, 0.09375, ((0, 16),))
    out_up = gaussian(splits[15], (R, D), R ** -0.5, 0.375, ((1, 16),))
    out_scale = gaussian(splits[16], (D,), 0.5, 3.0, ((0, 16),), jnp.float32)
    return {"tokens": tokens, "cotangent": cotangent, "norm_gain": norm_gain, "in_weight": in_weight, "in_down": in_down, "in_up": in_up, "in_scale": in_scale, "scale_table": scale_table, "table_pick": table_pick, "short_taps": short_taps, "residue": residue, "decay": decay, "skip_gain": skip_gain, "out_weight": out_weight, "out_down": out_down, "out_up": out_up, "out_scale": out_scale}


HIGH = lax.Precision.HIGHEST

def long_filter(residue, decay):
    steps = jnp.arange(L, dtype=jnp.int32)
    posf = steps.astype(jnp.float32)
    norm_fac = jnp.sqrt(-jnp.expm1(-2.0 * decay))
    return (residue * norm_fac)[:, None] * jnp.exp(-decay[:, None] * posf[None, :])

def reference(tokens, cotangent, norm_gain, in_weight, in_down, in_up, in_scale, scale_table, table_pick, short_taps, residue, decay, skip_gain, out_weight, out_down, out_up, out_scale):
    f32 = jnp.float32
    bf16 = jnp.bfloat16
    block = D // N_TP
    rim = TAPS - 1
    xf = tokens.astype(f32)
    rstd = lax.rsqrt(lax.optimization_barrier(jnp.sum(xf * xf, axis=1, keepdims=True)) / D + 1e-06)
    normed = (xf * rstd * norm_gain.astype(f32)[None, :]).astype(bf16)
    picked = scale_table[table_pick]
    low_in = jnp.dot(normed, in_down, preferred_element_type=f32)
    lowd = (low_in[None] * picked[:3, None, :]).astype(bf16)
    zlow = jnp.einsum('itr,ric->ict', lowd.astype(f32), in_up.astype(f32))
    zproj = jnp.einsum('td,dic->ict', normed.astype(f32), in_weight.astype(f32))
    z_all = (zproj + zlow * in_scale[:, :, None]).astype(bf16)
    padded = jnp.pad(z_all.astype(f32), ((0, 0), (0, 0), (rim, 0)))
    feat = jnp.zeros((3, D, L), f32)
    for tap in range(TAPS):
        feat = feat + short_taps[:, tap, :, None] * padded[:, :, rim - tap:rim - tap + L]
    query_part, key_part, value_part = (feat[0], feat[1], feat[2])
    product = (key_part * value_part).astype(bf16)
    filt = long_filter(residue, decay)
    spectrum = jnp.fft.rfft(filt, n=2 * L, axis=-1)
    conv = jnp.fft.irfft(jnp.fft.rfft(product.astype(f32), n=2 * L, axis=-1) * spectrum, n=2 * L, axis=-1)[:, :L]
    conv = conv.astype(f32).astype(bf16)
    mixsig = conv.astype(f32) + skip_gain[:, None] * product.astype(f32)
    gated = (query_part * mixsig).astype(bf16)
    low_out = jnp.einsum('ct,cr->tr', gated.astype(f32), out_down.astype(f32))
    lowd_out = (low_out * picked[3][None, :]).astype(bf16)
    olow = jnp.dot(lowd_out, out_up, preferred_element_type=f32)

    def out_group(index, total):
        rows = lax.dynamic_slice_in_dim(gated, (index * block).astype(jnp.int32), block, 0)
        weights = lax.dynamic_slice_in_dim(out_weight, (index * block).astype(jnp.int32), block, 0)
        part = jnp.dot(rows.T, weights, preferred_element_type=f32).astype(bf16)
        part = lax.optimization_barrier(part)
        return total + part.astype(f32)
    base_out = lax.fori_loop(0, N_TP, out_group, jnp.zeros((L, D), f32))
    mixed = (xf + base_out + olow * out_scale[None, :]).astype(bf16)
    cotf = cotangent.astype(f32)
    grad_out_scale = lax.optimization_barrier(jnp.sum(cotf * olow, axis=0))
    scaled_cot = (cotf * out_scale[None, :]).astype(bf16)
    dlowd_out = jnp.dot(scaled_cot, out_up.T, preferred_element_type=f32)
    grad_last = lax.optimization_barrier(jnp.sum(dlowd_out * low_out, axis=0))
    dlow_out = (dlowd_out * picked[3][None, :]).astype(bf16)
    dgated = jnp.einsum('ce,te->ct', out_weight.astype(f32), cotf) + jnp.einsum('cr,tr->ct', out_down.astype(f32), dlow_out.astype(f32))
    dquery = dgated * mixsig
    dmix = dgated * query_part
    dmix_b = dmix.astype(bf16)
    dconv = jnp.fft.irfft(jnp.conj(spectrum) * jnp.fft.rfft(dmix_b.astype(f32), n=2 * L, axis=-1), n=2 * L, axis=-1)[:, :L]
    dconv = dconv.astype(f32).astype(bf16)
    dprod = dconv.astype(f32) + skip_gain[:, None] * dmix
    dfeat = jnp.stack([dquery, dprod * value_part, dprod * key_part])
    extended = jnp.pad(dfeat, ((0, 0), (0, 0), (0, rim)))
    dz_all = jnp.zeros((3, D, L), f32)
    for tap in range(TAPS):
        dz_all = dz_all + short_taps[:, tap, :, None] * extended[:, :, tap:tap + L]
    grad_in_scale = lax.optimization_barrier(jnp.sum(dz_all * zlow, axis=2))
    dzs = (dz_all * in_scale[:, :, None]).astype(bf16)
    dlowd = jnp.einsum('ict,ric->itr', dzs.astype(f32), in_up.astype(f32))
    grad_first = lax.optimization_barrier(jnp.sum(dlowd * low_in[None], axis=1))
    dlow_in = lax.optimization_barrier(jnp.sum(dlowd * picked[:3, None, :], axis=0)).astype(bf16)
    dzb = dz_all.astype(bf16)

    def in_group(index, total):
        start = (index * block).astype(jnp.int32)
        weights = lax.dynamic_slice_in_dim(in_weight, start, block, 2)
        grads = lax.dynamic_slice_in_dim(dzb, start, block, 1)
        part = jnp.einsum('dic,ict->td', weights.astype(f32), grads.astype(f32)).astype(bf16)
        part = lax.optimization_barrier(part)
        return total + part.astype(f32)
    dnorm = lax.fori_loop(0, N_TP, in_group, jnp.zeros((L, D), f32))
    dnorm = dnorm + jnp.dot(dlow_in, in_down.T, preferred_element_type=f32)
    gdn = norm_gain.astype(f32)[None, :] * dnorm
    inner = lax.optimization_barrier(jnp.sum(xf * gdn, axis=1, keepdims=True))
    grad_tokens = (cotf + rstd * gdn - xf * rstd * rstd * rstd * inner / D).astype(bf16)
    onehot = (table_pick[:, None] == jnp.arange(G, dtype=jnp.int32)[None, :]).astype(f32)
    grad_rows = jnp.concatenate([grad_first, grad_last[None, :]], axis=0)
    grad_table = jnp.dot(onehot.T, grad_rows, precision=HIGH)
    return (mixed, grad_tokens, grad_table, grad_in_scale, grad_out_scale)
```

```python
import functools

import jax
import jax.numpy as jnp
from jax import lax
from jax.experimental import pallas as pl
from jax.experimental.pallas import tpu as pltpu
from jax.sharding import Mesh, PartitionSpec as P

HIGH = lax.Precision.HIGHEST
CTX = ("zl", "y", "core")
TP = ("x", "zh")
F32 = jnp.float32
BF16 = jnp.bfloat16
T = 256
C = 256
RANK = 256
SLABS = 16
WIDTH = 4096


def shift(v, axis, k):
    return lax.ppermute(v, axis, [(i, (i + k) % 4) for i in range(4)])


def exchange(v, axis):
    return [v] + [shift(v, axis, k) for k in (1, 3, 2)]


def ring_gather(g):
    left = shift(g, "x", 1)
    right = shift(g, "x", -1)
    half = g.shape[0] // 2
    far_a = shift(left[:half], "x", 1)
    far_b = shift(right[half:], "x", -1)
    return g, left, right, jnp.concatenate([far_a, far_b], 0)


def ring_scatter(own, to_right, to_left, far):
    half = far.shape[0] // 2
    ra = shift(far[:half], "x", 1).astype(F32)
    rb = shift(far[half:], "x", -1).astype(F32)
    to_right = jnp.concatenate(
        [(to_right[:half].astype(F32) + ra).astype(BF16), to_right[half:]], 0
    )
    to_left = jnp.concatenate(
        [to_left[:half], (to_left[half:].astype(F32) + rb).astype(BF16)], 0
    )
    r1 = shift(to_right, "x", 1)
    r3 = shift(to_left, "x", -1)
    total = (own.astype(F32) + r1.astype(F32) + r3.astype(F32)).astype(BF16)
    me = lax.axis_index("zh")
    acc = lax.dynamic_index_in_dim(total, me, 0, False).astype(F32)
    for k in (1, 3, 2):
        block = lax.dynamic_index_in_dim(total, (me + k) % 4, 0, False)
        acc = acc + shift(block, "zh", k).astype(F32)
    return acc


def split3(v):
    hi = lax.reduce_precision(v, 8, 7)
    rest = v - hi
    mid = lax.reduce_precision(rest, 8, 7)
    return jnp.concatenate([hi, mid, rest - mid], 0).astype(BF16)


def pack(main, rows):
    n = rows.shape[0]
    pad = jnp.zeros((16 - 3 * n, main.shape[1]), BF16)
    return jnp.concatenate([main.astype(BF16), split3(rows), pad], 0)


def sum_packed(parts, n):
    main = 0.0
    rows = 0.0
    for p in parts:
        main = main + p[:T].astype(F32)
        t = p[T : T + 3 * n].astype(F32)
        rows = rows + (t[:n] + t[n : 2 * n] + t[2 * n :])
    return main, rows


def reduce_packed(main, rows):
    n = rows.shape[0]
    for axis in ("x", "zh"):
        main, rows = sum_packed(exchange(pack(main, rows), axis), n)
    return main, rows


def reduce_plain(main):
    for axis in ("x", "zh"):
        parts = exchange(main.astype(BF16), axis)
        main = sum(p.astype(F32) for p in parts)
    return main


def ctx_gather(v):
    wide = jnp.broadcast_to(v[None], (SLABS,) + v.shape)
    return lax.all_to_all(wide, CTX, split_axis=0, concat_axis=0, tiled=True)


def dot(a, b):
    return jnp.dot(a, b, preferred_element_type=F32)


def dot_nt(a, b):
    return lax.dot_general(a, b, (((1,), (1,)), ((), ())), preferred_element_type=F32)


def rnd(v):
    return v.astype(BF16).astype(F32)


def row_ids():
    return lax.broadcasted_iota(jnp.int32, (T, C), 0)


def down(v, n, rows):
    return jnp.where(rows >= n, pltpu.roll(v, n, 0), 0.0)


def up(v, n, rows):
    return jnp.where(rows < T - n, pltpu.roll(v, T - n, 0), 0.0)


def scan_down(v, dec, rows):
    for k in range(8):
        n = 1 << k
        v = v + jnp.exp(-dec * n) * down(v, n, rows)
    return v


def scan_up(v, dec, rows):
    for k in range(8):
        n = 1 << k
        v = v + jnp.exp(-dec * n) * up(v, n, rows)
    return v


def fwd_in_kernel(
    idx, g0, g1, g2, g3, w0, w1, w2, w3, low_ref, rstd_ref, picked_ref, up_ref, scale_ref,
    taps_ref, kap_ref, dec_ref, zraw_ref, z_ref, zlow_ref, h_ref, edge_ref,
):
    j = pl.program_id(0)

    @pl.when(j == 0)
    def _():
        zraw_ref[...] = jnp.zeros_like(zraw_ref)

    for i in range(3):
        part = dot(g0[0], w0[i, 0])
        for g, w in ((g1, w1), (g2, w2), (g3, w3)):
            part = part + dot(g[0], w[i, 0])
        zraw_ref[i] += part

    @pl.when(j == 3)
    def _():
        rows = row_ids()
        rstd = rstd_ref[...]
        low_in = low_ref[...] * rstd
        feat = []
        for i in range(3):
            lowd = (low_in * picked_ref[i : i + 1, :]).astype(BF16)
            zlow = dot(lowd, up_ref[i])
            zlow_ref[i] = zlow
            z = (zraw_ref[i] * rstd + zlow * scale_ref[i : i + 1, :]).astype(BF16)
            z_ref[i] = z
            z = z.astype(F32)
            edge_ref[1 + 4 * i : 3 + 4 * i, :] = z[:2]
            edge_ref[3 + 4 * i : 5 + 4 * i, :] = z[T - 2 :]
            if i > 0:
                f = taps_ref[i, 0:1, :] * z
                for tap in (1, 2):
                    f = f + taps_ref[i, tap : tap + 1, :] * down(z, tap, rows)
                feat.append(f)
        dec = dec_ref[...]
        kap = kap_ref[...]
        u = jnp.where(rows >= 2, rnd(feat[0] * feat[1]), 0.0)
        h = scan_down(kap * u, dec, rows)
        h_ref[...] = h
        edge_ref[0:1, :] = h[T - 1 :]
        edge_ref[13:16, :] = jnp.zeros((3, C), F32)


def fwd_out_kernel(
    idx, edges_ref, z_ref, h_ref, taps_ref, kap_ref, dec_ref, skip_ref, down_ref, ow_ref,
    part_ref, low_ref, q_ref, k_ref, v_ref, mix_ref, next_ref, gated_ref,
):
    j = pl.program_id(0)

    @pl.when(j == 0)
    def _():
        me = idx[4]
        rows = row_ids()
        dec = dec_ref[...]
        kap = kap_ref[...]
        skip = skip_ref[...]
        slab = lax.broadcasted_iota(jnp.int32, (SLABS, C), 0)

        def edge(r):
            return edges_ref[:, r, :]

        def prev(v):
            return jnp.where(slab >= 1, pltpu.roll(v, 1, 0), 0.0)

        def own(v):
            return jnp.sum(jnp.where(slab == me, v, 0.0), axis=0, keepdims=True)

        def following(v):
            return jnp.sum(jnp.where(slab == me + 1, v, 0.0), axis=0, keepdims=True)

        first0, first1, full, halo = [], [], [], []
        for i in range(3):
            t0, t1, t2 = (taps_ref[i, n : n + 1, :] for n in range(3))
            a0, a1 = edge(1 + 4 * i), edge(2 + 4 * i)
            b0, b1 = prev(edge(3 + 4 * i)), prev(edge(4 + 4 * i))
            first0.append(t0 * a0 + t1 * b1 + t2 * b0)
            first1.append(t0 * a1 + t1 * a0 + t2 * b1)
            p0, p1 = own(b0), own(b1)
            z = z_ref[i].astype(F32)
            s1 = jnp.where(rows == 0, p1, pltpu.roll(z, 1, 0))
            s2 = jnp.where(rows == 0, p0, jnp.where(rows == 1, p1, pltpu.roll(z, 2, 0)))
            full.append(t0 * z + t1 * s1 + t2 * s2)
        u0 = rnd(first0[1] * first0[2])
        u1 = rnd(first1[1] * first1[2])
        total = edge(0) + kap * (jnp.exp(-dec * (T - 1)) * u0 + jnp.exp(-dec * (T - 2)) * u1)
        ahead = (me - 1 - slab).astype(F32)
        weight = jnp.exp(-dec * (T * jnp.maximum(ahead, 0.0)))
        carry = jnp.sum(jnp.where(slab < me, weight * total, 0.0), axis=0, keepdims=True)
        carry_next = jnp.exp(-dec * T) * carry + own(total)
        one = jnp.exp(-dec)
        power = jnp.exp(-dec * rows.astype(F32))
        bump = jnp.where(rows >= 1, kap * own(u1) * jnp.exp(dec), 0.0)
        h = h_ref[...] + power * (one * carry + kap * own(u0) + bump)
        q, kf, vf = full
        mix = rnd(h) + skip * rnd(kf * vf)
        gated = (q * mix).astype(BF16)
        gated_ref[...] = gated
        q_ref[...] = q
        k_ref[...] = kf
        v_ref[...] = vf
        mix_ref[...] = mix
        n0 = following(u0)
        n1 = following(u1)
        h0 = one * carry_next + kap * n0
        h1 = one * h0 + kap * n1
        next_ref[0:1, :] = rnd(h0) + skip * n0
        next_ref[1:2, :] = rnd(h1) + skip * n1
        for i in range(3):
            next_ref[2 + 2 * i : 3 + 2 * i, :] = following(first0[i])
            next_ref[3 + 2 * i : 4 + 2 * i, :] = following(first1[i])
        low_ref[...] = dot(gated, down_ref[...]).astype(BF16)

    part_ref[0] = dot(gated_ref[...], ow_ref[...]).astype(BF16)


def bwd_in_kernel(
    idx, g0, g1, g2, g3, w0, w1, w2, w3, dlow_ref, picked_ref, down_ref, q_ref, kap_ref, dec_ref,
    dg_ref, gsum_ref, edge_ref,
):
    j = pl.program_id(0)

    @pl.when(j == 0)
    def _():
        dlow = (dlow_ref[...] * picked_ref[3:4, :]).astype(BF16)
        dg_ref[...] = dot_nt(dlow, down_ref[...])

    part = dot_nt(g0[0], w0[...])
    for g, w in ((g1, w1), (g2, w2), (g3, w3)):
        part = part + dot_nt(g[0], w[...])
    dg_ref[...] += part

    @pl.when(j == 3)
    def _():
        rows = row_ids()
        dec = dec_ref[...]
        kap = kap_ref[...]
        dg = dg_ref[...]
        g = scan_up(kap * rnd(dg * q_ref[...]), dec, rows)
        gsum_ref[...] = g
        edge_ref[0:2, :] = g[:2]
        edge_ref[2:4, :] = dg[:2]
        edge_ref[4:8, :] = jnp.zeros((4, C), F32)


def bwd_out_kernel(
    idx, edges_ref, dg_ref, g_ref, q_ref, k_ref, v_ref, mix_ref, next_ref, taps_ref, dec_ref,
    skip_ref, zraw_ref, zlow_ref, low_ref, rstd_ref, picked_ref, scale_ref, up_ref, w_ref,
    part_ref, dlow_ref, inner_ref, rows_ref, dzb_ref,
):
    j = pl.program_id(0)

    @pl.when(j == 0)
    def _():
        me = idx[4]
        rows = row_ids()
        dec = dec_ref[...]
        skip = skip_ref[...]
        slab = lax.broadcasted_iota(jnp.int32, (SLABS, C), 0)

        def following(v):
            return jnp.sum(jnp.where(slab == me + 1, v, 0.0), axis=0, keepdims=True)

        head = edges_ref[:, 0, :]
        ahead = (slab - me - 1).astype(F32)
        weight = jnp.exp(-dec * (T * jnp.maximum(ahead, 0.0)))
        carry = jnp.sum(jnp.where(slab > me, weight * head, 0.0), axis=0, keepdims=True)
        weight = jnp.exp(-dec * (T * jnp.maximum(ahead - 1.0, 0.0)))
        carry_next = jnp.sum(jnp.where(slab > me + 1, weight * head, 0.0), axis=0, keepdims=True)
        g = g_ref[...] + jnp.exp(-dec * (T - rows).astype(F32)) * carry
        dg = dg_ref[...]
        q, kf, vf = q_ref[...], k_ref[...], v_ref[...]
        dprod = rnd(g) + skip * (dg * q)
        dfeat = (dg * mix_ref[...], dprod * vf, dprod * kf)
        dg0 = following(edges_ref[:, 2, :])
        dg1 = following(edges_ref[:, 3, :])
        g1 = following(edges_ref[:, 1, :]) + jnp.exp(-dec * (T - 1)) * carry_next
        nxt = [next_ref[n : n + 1, :] for n in range(8)]
        dp0 = rnd(carry) + skip * (dg0 * nxt[2])
        dp1 = rnd(g1) + skip * (dg1 * nxt[3])
        inside = (jnp.full((1, C), me, jnp.int32) < SLABS - 1)
        after0 = [jnp.where(inside, v, 0.0) for v in (dg0 * nxt[0], dp0 * nxt[6], dp0 * nxt[4])]
        after1 = [jnp.where(inside, v, 0.0) for v in (dg1 * nxt[1], dp1 * nxt[7], dp1 * nxt[5])]
        low_raw = low_ref[...]
        low_in = low_raw * rstd_ref[...]
        dlow = jnp.zeros((T, RANK), F32)
        inner = jnp.zeros((T, C), F32)
        for i in range(3):
            t0, t1, t2 = (taps_ref[i, n : n + 1, :] for n in range(3))
            d = dfeat[i]
            s1 = jnp.where(rows == T - 1, after0[i], pltpu.roll(d, T - 1, 0))
            s2 = jnp.where(
                rows == T - 2, after0[i], jnp.where(rows == T - 1, after1[i], pltpu.roll(d, T - 2, 0))
            )
            dz = t0 * d + t1 * s1 + t2 * s2
            dzb_ref[i] = dz.astype(BF16)
            rows_ref[i : i + 1, :] = jnp.sum(dz * zlow_ref[i], axis=0, keepdims=True)
            dzs = (dz * scale_ref[i : i + 1, :]).astype(BF16)
            dlowd = dot_nt(dzs, up_ref[i])
            rows_ref[3 + i : 4 + i, :] = jnp.sum(dlowd * low_in, axis=0, keepdims=True)
            dlow = dlow + dlowd * picked_ref[i : i + 1, :]
            inner = inner + dz * zraw_ref[i]
        rows_ref[6:8, :] = jnp.zeros((2, C), F32)
        dlow_ref[...] = dlow.astype(BF16)
        inner_ref[...] = jnp.sum(inner + dlow * low_raw, axis=1, keepdims=True)

    acc = dot_nt(dzb_ref[0], w_ref[0, 0])
    acc = acc + dot_nt(dzb_ref[1], w_ref[1, 0])
    acc = acc + dot_nt(dzb_ref[2], w_ref[2, 0])
    part_ref[0] = acc.astype(BF16)


def whole(shape):
    zero = (0,) * len(shape)
    return pl.BlockSpec(shape, lambda j, idx: zero)


def call(kernel, grid, in_specs, out_specs, out_shape, scratch, flops, bytes_accessed):
    return pl.pallas_call(
        kernel,
        out_shape=out_shape,
        grid_spec=pltpu.PrefetchScalarGridSpec(
            num_scalar_prefetch=1,
            grid=(grid,),
            in_specs=in_specs,
            out_specs=out_specs,
            scratch_shapes=scratch,
        ),
        compiler_params=pltpu.CompilerParams(vmem_limit_bytes=40 * 2**20),
        cost_estimate=pl.CostEstimate(
            flops=flops, bytes_accessed=bytes_accessed, transcendentals=0
        ),
    )


def sds(shape, dtype):
    return jax.ShapeDtypeStruct(shape, dtype)


def on_device(
    tokens,
    cotangent,
    norm_gain,
    in_weight,
    in_down,
    in_up,
    in_scale,
    scale_table,
    table_pick,
    short_taps,
    residue,
    decay,
    skip_gain,
    out_weight,
    out_down,
    out_up,
    out_scale,
):
    groups = scale_table.shape[0]
    onehot = (table_pick[:, None] == jnp.arange(groups, dtype=jnp.int32)[None, :]).astype(F32)
    picked = jnp.dot(onehot, scale_table, precision=HIGH)
    me_x = lax.axis_index("x")
    me_ctx = lax.axis_index(CTX)
    idx = jnp.stack([me_x, (me_x + 3) % 4, (me_x + 1) % 4, (me_x + 2) % 4, me_ctx]).astype(jnp.int32)
    weight = jnp.transpose(in_weight, (1, 0, 2)).reshape(3, 16, 256, C)
    up_in = jnp.transpose(in_up, (1, 0, 2))
    kap = (residue * jnp.sqrt(-jnp.expm1(-2.0 * decay)))[None]
    dec, skip = decay[None], skip_gain[None]

    xf = tokens.astype(F32)
    gainf = norm_gain.astype(F32)
    cotf = cotangent.astype(F32)
    xg = (xf * gainf[None, :]).astype(BF16)
    xg_z = lax.all_gather(xg, "zh")
    cot_z = lax.all_gather(cotangent, "zh")
    squares = jnp.sum(xf * xf, axis=1)[None]
    low_part = dot(xg, in_down)
    scaled_cot = (cotf * out_scale[None, :]).astype(BF16)
    dl_part = dot_nt(scaled_cot, out_up)
    low_raw, squares = reduce_packed(low_part, squares)
    rstd = lax.rsqrt(squares / WIDTH + 1e-06).reshape(T, 1)
    xs = ring_gather(xg_z)
    dlowd_out = reduce_plain(dl_part)
    cs = ring_gather(cot_z)

    def gathered():
        return [pl.BlockSpec((1, T, 256), lambda j, idx: (j, 0, 0)) for _ in range(4)]

    def in_blocks(k):
        return pl.BlockSpec((3, 1, 256, C), lambda j, idx: (0, idx[k] * 4 + j, 0, 0))

    def out_blocks(k):
        return pl.BlockSpec((C, 256), lambda j, idx: (0, idx[k] * 4 + j))

    row = whole((1, C))
    square = whole((T, C))
    triple = whole((3, T, C))
    taps_spec = whole((3, 3, C))
    col = whole((T, 1))
    picked_spec = whole((4, RANK))
    scale_spec = whole((3, C))
    zraw, z, zlow, h, edge = call(
        fwd_in_kernel,
        4,
        gathered() + [in_blocks(k) for k in range(4)]
        + [square, col, picked_spec, triple, scale_spec, taps_spec, row, row],
        [triple, triple, triple, square, whole((16, C))],
        [sds((3, T, C), F32), sds((3, T, C), BF16), sds((3, T, C), F32), sds((T, C), F32), sds((16, C), F32)],
        [],
        2 * T * WIDTH * 3 * C,
        9 << 20,
    )(idx, *xs, *([weight] * 4), low_raw, rstd, picked, up_in, in_scale, short_taps, kap, dec)
    edges = ctx_gather(edge)

    def rel(j, idx):
        return idx[j // 4] * 4 + j % 4

    parts, low_out_part, q, kf, vf, mix, nxt = call(
        fwd_out_kernel,
        16,
        [whole((SLABS, 16, C)), triple, square, taps_spec, row, row, row, whole((C, RANK)),
         pl.BlockSpec((C, 256), lambda j, idx: (0, rel(j, idx)))],
        [pl.BlockSpec((1, T, 256), lambda j, idx: (j, 0, 0)), square, square, square, square, square, whole((8, C))],
        [sds((16, T, 256), BF16), sds((T, RANK), BF16)] + [sds((T, C), F32)] * 4 + [sds((8, C), F32)],
        [pltpu.VMEM((T, C), BF16)],
        2 * T * WIDTH * C,
        6 << 20,
    )(idx, edges, z, h, short_taps, kap, dec, skip, out_down, out_weight)
    base_out = ring_scatter(parts[0:4], parts[8:12], parts[4:8], parts[12:16])
    low_out = reduce_plain(low_out_part)

    dg, gsum, gedge = call(
        bwd_in_kernel,
        4,
        gathered() + [out_blocks(k) for k in range(4)]
        + [square, picked_spec, whole((C, RANK)), square, row, row],
        [square, square, whole((8, C))],
        [sds((T, C), F32), sds((T, C), F32), sds((8, C), F32)],
        [],
        2 * T * WIDTH * C,
        5 << 20,
    )(idx, *cs, *([out_weight] * 4), dlowd_out, picked, out_down, q, kap, dec)
    gedges = ctx_gather(gedge)

    dparts, dlow_part, inner_part, sums = call(
        bwd_out_kernel,
        16,
        [whole((SLABS, 8, C)), square, square, square, square, square, square, whole((8, C)),
         taps_spec, row, row, triple, triple, square, col, picked_spec, scale_spec, triple,
         pl.BlockSpec((3, 1, 256, C), lambda j, idx: (0, rel(j, idx), 0, 0))],
        [pl.BlockSpec((1, T, 256), lambda j, idx: (j, 0, 0)), square, col, whole((8, C))],
        [sds((16, T, 256), BF16), sds((T, RANK), BF16), sds((T, 1), F32), sds((8, C), F32)],
        [pltpu.VMEM((3, T, C), BF16)],
        2 * T * WIDTH * 3 * C,
        12 << 20,
    )(idx, gedges, dg, gsum, q, kf, vf, mix, nxt, short_taps, dec, skip, zraw, zlow, low_raw,
      rstd, picked, in_scale, up_in, weight)
    dlow_sum, tail = reduce_packed(
        dlow_part, jnp.concatenate([inner_part.reshape(1, T), sums[3:6]], 0)
    )
    dnorm = ring_scatter(dparts[0:4], dparts[8:12], dparts[4:8], dparts[12:16])

    lowd_out = (low_out * picked[3][None, :]).astype(BF16)
    olow = dot(lowd_out, out_up)
    mixed = (xf + base_out + olow * out_scale[None, :]).astype(BF16)
    gos_part = jnp.sum(cotf * olow, axis=0)
    grad_last = jnp.sum(dlowd_out * low_out, axis=0)
    report = jnp.concatenate([sums[:3], gos_part[None], tail[1:4], grad_last[None]], 0)
    report = jnp.sum(ctx_gather(report), axis=0)
    grad_in_scale = report[:3]
    grad_out_scale = report[3]
    grad_table = jnp.dot(onehot.T, report[4:8], precision=HIGH)

    dlow_in = dlow_sum.astype(BF16)
    dnorm = dnorm + dot_nt(dlow_in, in_down)
    inner = tail[0].reshape(T, 1)
    grad_tokens = (
        cotf + rstd * (gainf[None, :] * dnorm) - xf * (rstd * rstd * rstd * inner / WIDTH)
    ).astype(BF16)
    return (mixed, grad_tokens, grad_table, grad_in_scale, grad_out_scale)


def solution(mesh):
    fine = Mesh(mesh.devices.reshape(2, 4, 2, 4, 4), CTX + TP)
    return jax.shard_map(
        on_device,
        mesh=fine,
        in_specs=(
            P(CTX, TP),
            P(CTX, TP),
            P(TP),
            P(None, None, TP),
            P(TP, None),
            P(None, None, TP),
            P(None, TP),
            P(),
            P(),
            P(None, None, TP),
            P(TP),
            P(TP),
            P(TP),
            P(TP, None),
            P(TP, None),
            P(None, TP),
            P(TP),
        ),
        out_specs=(P(CTX, TP), P(CTX, TP), P(), P(None, TP), P(TP)),
        check_vma=False,
    )
```

```python
import jax
import jax.numpy as jnp
from jax import lax
from jax.experimental import pallas as pl
from jax.experimental.pallas import tpu as pltpu
from jax.sharding import Mesh, PartitionSpec as P

HIGH = lax.Precision.HIGHEST
CTX = ("zl", "y", "core")
TP = ("x", "zh")
F32 = jnp.float32
BF16 = jnp.bfloat16
T = 256
C = 256
RANK = 256
SLABS = 16
WIDTH = 4096
KAP, DEC, SKIP, SCALE, TAPS, PICKED = 0, 1, 2, 3, 6, 15
LOW_T = 272
CUT_T = 144
CUT = 128


def shift(v, axis, k):
    return lax.ppermute(v, axis, [(i, (i + k) % 4) for i in range(4)])


def swap(v, axis):
    return lax.ppermute(v, axis, [(0, 1), (1, 0)])


def stack(*parts):
    def kernel(*refs):
        for i, ref in enumerate(refs[:-1]):
            refs[-1][i] = ref[...]

    return call(kernel, [((len(parts),) + parts[0].shape, parts[0].dtype)], parts)[0]


def ctx_gather(v):
    pair = stack(v, swap(v, "core"))
    quad = stack(pair, *[shift(pair, "y", k) for k in (1, 2, 3)])
    return quad, swap(quad, "zl")


def across(v, axis, bit):
    return lax.ppermute(v, axis, [(i, i ^ bit) for i in range(4)])


def ctx_sum(v):
    v = v + swap(v, "core")
    v = v + swap(v, "zl")
    return v + shift(v, "y", 1) + shift(v, "y", 2) + shift(v, "y", 3)


def place(scr, near, other):
    zl, y, core = (lax.axis_index(a) for a in CTX)
    for kz, src in enumerate((near, other)):
        for ky in range(4):
            for kc in range(2):
                slab = (1 - zl if kz else zl) * 8 + lax.rem(y + 4 - ky, 4) * 2
                slab = slab + (1 - core if kc else core)
                scr[slab] = src[ky, kc]


def position():
    zl, y, core = (lax.axis_index(a) for a in CTX)
    return zl * 8 + y * 2 + core


def block_ids():
    x, zh = lax.axis_index("x"), lax.axis_index("zh")
    xs = [x, lax.rem(x + 3, 4), lax.rem(x + 1, 4), lax.rem(x + 2, 4)]
    zs = [jnp.bitwise_xor(zh, r) for r in range(4)]
    return [[a * 4 + b for b in zs] for a in xs]


def ring_gather(own, cut):
    left, right = shift(own, "x", 1), shift(own, "x", -1)
    rows = own.shape[0]

    def kernel(left_ref, right_ref, fa, fb):
        fa[...] = left_ref[0:cut, :]
        fb[...] = right_ref[cut:rows, :]

    shapes = [((cut, C), BF16), ((rows - cut, C), BF16)]
    fa, fb = call(kernel, shapes, [left, right])
    return [own, left, right, shift(fa, "x", 1), shift(fb, "x", -1)], fa


def as_pairs(quad, cut):
    own, left, right, fa, fb = quad
    rows = own.shape[0]
    out = [(g.at[0:cut, :], g.at[cut:rows, :]) for g in (own, left, right)]
    return out + [(fa, fb)]


def dot(a, b):
    return jnp.dot(a, b, preferred_element_type=F32)


def dot_nt(a, b):
    return lax.dot_general(a, b, (((1,), (1,)), ((), ())), preferred_element_type=F32)


def rnd(v):
    return v.astype(BF16).astype(F32)


def row_ids():
    return lax.broadcasted_iota(jnp.int32, (T, C), 0)


def column(row):
    square = (T, T)
    same = lax.broadcasted_iota(jnp.int32, square, 0) == lax.broadcasted_iota(jnp.int32, square, 1)
    return jnp.sum(jnp.where(same, row, 0.0), axis=1, keepdims=True)


def line(col):
    square = (T, T)
    same = lax.broadcasted_iota(jnp.int32, square, 0) == lax.broadcasted_iota(jnp.int32, square, 1)
    return jnp.sum(jnp.where(same, col, 0.0), axis=0, keepdims=True)


def thirds(row):
    hi = rnd(row)
    mid = rnd(row - hi)
    return [hi, mid, row - hi - mid]


def tile_of(rows, n=16):
    at = lax.broadcasted_iota(jnp.int32, (n, C), 0)
    out = jnp.zeros((n, C), F32)
    for i, row in enumerate(rows):
        out = jnp.where(at == i, row, out)
    return out.astype(BF16)


def joined(tile, i):
    return tile[i : i + 1] + tile[i + 1 : i + 2] + tile[i + 2 : i + 3]


def down(v, n, rows):
    return jnp.where(rows >= n, pltpu.roll(v, n, 0), 0.0)


def up(v, n, rows):
    return jnp.where(rows < T - n, pltpu.roll(v, T - n, 0), 0.0)


def scan_down(v, dec, rows):
    for k in range(8):
        n = 1 << k
        v = v + jnp.exp(-dec * n) * down(v, n, rows)
    return v


def scan_up(v, dec, rows):
    for k in range(8):
        n = 1 << k
        v = v + jnp.exp(-dec * n) * up(v, n, rows)
    return v


def row_of(ref, n):
    return ref[n : n + 1, :]


def blk(a_ref, b_ref, r, head):
    if r < 2:
        return a_ref[r * 256 : r * 256 + 256, :]
    at = head + (r - 2) * 256
    return b_ref[at : at + 256, :]


def put_blk(a_ref, b_ref, r, head, v):
    if r < 2:
        a_ref[r * 256 : r * 256 + 256, :] = v
    else:
        at = head + (r - 2) * 256
        b_ref[at : at + 256, :] = v


def low_sum(pairs, cut, low):
    out = []
    for part, size in ((0, cut), (1, low - cut)):
        at = 512 if part == 0 else 0
        v = 0.0
        for pair in pairs:
            v = v + pair[part][at : at + size, :].astype(F32)
        out.append(v)
    return jnp.concatenate(out, 0)


def const_kernel(pick, kap, dec, skip, scale, taps, table, cst):
    cst[0:1, :] = kap[...]
    cst[1:2, :] = dec[...]
    cst[2:3, :] = skip[...]
    cst[3:6, :] = scale[...]
    for i in range(3):
        for j in range(3):
            cst[TAPS + 3 * i + j : TAPS + 3 * i + j + 1, :] = taps[i, j : j + 1, :]
    for i in range(4):
        row = jnp.zeros((1, RANK), F32)
        for g in range(4):
            chosen = jnp.full((1, RANK), pick[i], jnp.int32) == g
            row = row + jnp.where(chosen, table[g : g + 1, :], 0.0)
        cst[PICKED + i : PICKED + i + 1, :] = row
    cst[19:24, :] = jnp.zeros((5, C), F32)


def cot_start_kernel(cot, upw, scale, after, pay):
    pay[0:256, :] = cot[...]
    pay[256:512, :] = upw[...]
    at = lax.broadcasted_iota(jnp.int32, (16, C), 0)
    rows = after[512:528, :].astype(F32)
    for i, row in enumerate(thirds(scale[...])):
        rows = jnp.where(at == i, row, rows)
    pay[512:528, :] = rows.astype(BF16)


def token_kernel(z0, z1, z2, z3, out):
    a_ref, b_ref = out.at[0:656, :], out.at[656:1296, :]
    low = jnp.zeros((T, RANK), F32)
    squares = jnp.zeros((T, 1), F32)
    for r, z in enumerate((z0, z1, z2, z3)):
        x = z[:256, :].astype(F32)
        gain = z[512:528, :].astype(F32)[:1]
        xg = (x * gain).astype(BF16)
        put_blk(a_ref, b_ref, r, 128, xg)
        low = low + dot(xg, z[256:512, :])
        squares = squares + jnp.sum(x * x, axis=1, keepdims=True)
    low = low.astype(BF16)
    a_ref[512:656, :] = low[:144]
    b_ref[0:112, :] = low[144:]
    b_ref[112:128, :] = tile_of(thirds(line(squares)))


def cot_kernel(z0, z1, z2, z3, out):
    a_ref, b_ref = out.at[0:640, :], out.at[640:1280, :]
    low = jnp.zeros((T, RANK), F32)
    for r, z in enumerate((z0, z1, z2, z3)):
        cot = z[:256, :]
        scale = joined(z[512:528, :].astype(F32), 0)
        put_blk(a_ref, b_ref, r, 128, cot)
        low = low + dot_nt((cot.astype(F32) * scale).astype(BF16), z[256:512, :])
    low = low.astype(BF16)
    a_ref[512:640, :] = low[:128]
    b_ref[0:128, :] = low[128:]


def fwd_in_kernel(
    g0, g1, g2, ga, gb, w_ref, up_ref, cst,
    zraw_ref, z_ref, zlow_ref, h_ref, edge_ref, low_ref, rstd_ref,
):
    rows = row_ids()
    ids = block_ids()
    pairs = as_pairs((g0, g1, g2, ga, gb), 656)
    total = low_sum(pairs, CUT_T, LOW_T)
    rstd = column(lax.rsqrt(joined(total[256:], 0) / WIDTH + 1e-06))
    rstd_ref[...] = rstd
    low_ref[...] = total[:256]
    low_in = low_ref[...] * rstd
    dec = row_of(cst, DEC)
    feat = []
    for i in range(3):
        acc = jnp.zeros((T, C), F32)
        for k, pair in enumerate(pairs):
            for r in range(4):
                acc = acc + dot(blk(*pair, r, 128), w_ref[i, ids[k][r]])
        zraw_ref[i] = acc
        zlow = dot((low_in * row_of(cst, PICKED + i)).astype(BF16), up_ref[i])
        zlow_ref[i] = zlow
        z = (acc * rstd + zlow * row_of(cst, SCALE + i)).astype(BF16)
        z_ref[i] = z
        z = z.astype(F32)
        edge_ref[1 + 4 * i : 3 + 4 * i, :] = z[:2]
        edge_ref[3 + 4 * i : 5 + 4 * i, :] = z[T - 2 :]
        if i > 0:
            f = row_of(cst, TAPS + 3 * i) * z
            for tap in (1, 2):
                f = f + row_of(cst, TAPS + 3 * i + tap) * down(z, tap, rows)
            feat.append(f)
    u = jnp.where(rows >= 2, rnd(feat[0] * feat[1]), 0.0)
    h = scan_down(row_of(cst, KAP) * u, dec, rows)
    h_ref[...] = h
    edge_ref[0:1, :] = h[T - 1 :]
    edge_ref[13:16, :] = jnp.zeros((3, C), F32)


def fwd_out_kernel(
    near, other, z_ref, h_ref, cst,
    gated_ref, q_ref, k_ref, v_ref, mix_ref, next_ref, edges_ref,
):
    me = position()
    place(edges_ref, near, other)
    rows = row_ids()
    dec = row_of(cst, DEC)
    kap = row_of(cst, KAP)
    skip = row_of(cst, SKIP)
    slab = lax.broadcasted_iota(jnp.int32, (SLABS, C), 0)

    def edge(r):
        return edges_ref[:, r, :]

    def prev(v):
        return jnp.where(slab >= 1, pltpu.roll(v, 1, 0), 0.0)

    def own(v):
        return jnp.sum(jnp.where(slab == me, v, 0.0), axis=0, keepdims=True)

    def following(v):
        return jnp.sum(jnp.where(slab == me + 1, v, 0.0), axis=0, keepdims=True)

    first0, first1, full = [], [], []
    for i in range(3):
        t0, t1, t2 = (row_of(cst, TAPS + 3 * i + n) for n in range(3))
        a0, a1 = edge(1 + 4 * i), edge(2 + 4 * i)
        b0, b1 = prev(edge(3 + 4 * i)), prev(edge(4 + 4 * i))
        first0.append(t0 * a0 + t1 * b1 + t2 * b0)
        first1.append(t0 * a1 + t1 * a0 + t2 * b1)
        p0, p1 = own(b0), own(b1)
        z = z_ref[i].astype(F32)
        s1 = jnp.where(rows == 0, p1, pltpu.roll(z, 1, 0))
        s2 = jnp.where(rows == 0, p0, jnp.where(rows == 1, p1, pltpu.roll(z, 2, 0)))
        full.append(t0 * z + t1 * s1 + t2 * s2)
    u0 = rnd(first0[1] * first0[2])
    u1 = rnd(first1[1] * first1[2])
    total = edge(0) + kap * (jnp.exp(-dec * (T - 1)) * u0 + jnp.exp(-dec * (T - 2)) * u1)
    ahead = (me - 1 - slab).astype(F32)
    weight = jnp.exp(-dec * (T * jnp.maximum(ahead, 0.0)))
    carry = jnp.sum(jnp.where(slab < me, weight * total, 0.0), axis=0, keepdims=True)
    carry_next = jnp.exp(-dec * T) * carry + own(total)
    one = jnp.exp(-dec)
    power = jnp.exp(-dec * rows.astype(F32))
    bump = jnp.where(rows >= 1, kap * own(u1) * jnp.exp(dec), 0.0)
    h = h_ref[...] + power * (one * carry + kap * own(u0) + bump)
    q, kf, vf = full
    mix = rnd(h) + skip * rnd(kf * vf)
    gated_ref[...] = (q * mix).astype(BF16)
    q_ref[...] = q
    k_ref[...] = kf
    v_ref[...] = vf
    mix_ref[...] = mix
    n0 = following(u0)
    n1 = following(u1)
    h0 = one * carry_next + kap * n0
    h1 = one * h0 + kap * n1
    next_ref[0:1, :] = rnd(h0) + skip * n0
    next_ref[1:2, :] = rnd(h1) + skip * n1
    for i in range(3):
        next_ref[2 + 2 * i : 3 + 2 * i, :] = following(first0[i])
        next_ref[3 + 2 * i : 4 + 2 * i, :] = following(first1[i])


def part_kernel(gated_ref, down_ref, ow_ref, fa_ref, fb_ref, right_ref, left_ref, own_ref):
    ids = block_ids()
    gated = gated_ref[...]
    low = dot(gated, down_ref[...]).astype(BF16)
    fa_ref[512:768, :] = low
    fb_ref[512:768, :] = low
    for k, dst in ((3, None), (2, right_ref), (1, left_ref), (0, own_ref)):
        for r in range(4):
            cols = pl.ds(pl.multiple_of(ids[k][r] * 256, 256), 256)
            part = dot(gated, ow_ref[:, cols]).astype(BF16)
            if dst is None:
                half = fa_ref if r < 2 else fb_ref
                half[(r % 2) * 256 : (r % 2) * 256 + 256, :] = part
            else:
                dst[r * 256 : r * 256 + 256, :] = part


def bwd_in_kernel(
    g0, g1, g2, ga, gb, ow_ref, down_ref, q_ref, fa_out, cst,
    dg_ref, gsum_ref, edge_ref, last_ref,
):
    rows = row_ids()
    dec = row_of(cst, DEC)
    ids = block_ids()
    pairs = as_pairs((g0, g1, g2, ga, gb), 640)
    dlowd = low_sum(pairs, CUT, 256)
    last = jnp.sum(dlowd * fa_out[512:768, :].astype(F32), axis=0, keepdims=True)
    last_ref[...] = jnp.broadcast_to(last, (8, RANK))
    dg = dot_nt((dlowd * row_of(cst, PICKED + 3)).astype(BF16), down_ref[...])
    for k, pair in enumerate(pairs):
        for r in range(4):
            cols = pl.ds(pl.multiple_of(ids[k][r] * 256, 256), 256)
            dg = dg + dot_nt(blk(*pair, r, 128), ow_ref[:, cols])
    dg_ref[...] = dg
    g = scan_up(row_of(cst, KAP) * rnd(dg * q_ref[...]), dec, rows)
    gsum_ref[...] = g
    edge_ref[0:2, :] = g[:2]
    edge_ref[2:4, :] = dg[:2]
    edge_ref[4:8, :] = jnp.zeros((4, C), F32)


def bwd_out_kernel(
    near, other, dg_ref, g_ref, q_ref, k_ref, v_ref, mix_ref, next_ref, cst, zraw_ref,
    zlow_ref, low_ref, rstd_ref, last_ref, up_ref, w_ref,
    fa_ref, fb_ref, right_ref, left_ref, own_ref, rows_ref, dzb_ref, edges_ref,
):
    me = position()
    ids = block_ids()
    place(edges_ref, near, other)
    rows = row_ids()
    dec = row_of(cst, DEC)
    skip = row_of(cst, SKIP)
    slab = lax.broadcasted_iota(jnp.int32, (SLABS, C), 0)

    def following(v):
        return jnp.sum(jnp.where(slab == me + 1, v, 0.0), axis=0, keepdims=True)

    head = edges_ref[:, 0, :]
    ahead = (slab - me - 1).astype(F32)
    weight = jnp.exp(-dec * (T * jnp.maximum(ahead, 0.0)))
    carry = jnp.sum(jnp.where(slab > me, weight * head, 0.0), axis=0, keepdims=True)
    weight = jnp.exp(-dec * (T * jnp.maximum(ahead - 1.0, 0.0)))
    carry_next = jnp.sum(jnp.where(slab > me + 1, weight * head, 0.0), axis=0, keepdims=True)
    g = g_ref[...] + jnp.exp(-dec * (T - rows).astype(F32)) * carry
    dg = dg_ref[...]
    q, kf, vf = q_ref[...], k_ref[...], v_ref[...]
    dprod = rnd(g) + skip * (dg * q)
    dfeat = (dg * mix_ref[...], dprod * vf, dprod * kf)
    dg0 = following(edges_ref[:, 2, :])
    dg1 = following(edges_ref[:, 3, :])
    g1 = following(edges_ref[:, 1, :]) + jnp.exp(-dec * (T - 1)) * carry_next
    nxt = [row_of(next_ref, n) for n in range(8)]
    dp0 = rnd(carry) + skip * (dg0 * nxt[2])
    dp1 = rnd(g1) + skip * (dg1 * nxt[3])
    inside = jnp.full((1, C), me, jnp.int32) < SLABS - 1
    after0 = [jnp.where(inside, v, 0.0) for v in (dg0 * nxt[0], dp0 * nxt[6], dp0 * nxt[4])]
    after1 = [jnp.where(inside, v, 0.0) for v in (dg1 * nxt[1], dp1 * nxt[7], dp1 * nxt[5])]
    low_raw = low_ref[...]
    low_in = low_raw * rstd_ref[...]
    dlow = jnp.zeros((T, RANK), F32)
    inner = jnp.zeros((T, C), F32)
    grads = []
    for i in range(3):
        t0, t1, t2 = (row_of(cst, TAPS + 3 * i + n) for n in range(3))
        d = dfeat[i]
        s1 = jnp.where(rows == T - 1, after0[i], pltpu.roll(d, T - 1, 0))
        s2 = jnp.where(
            rows == T - 2, after0[i], jnp.where(rows == T - 1, after1[i], pltpu.roll(d, T - 2, 0))
        )
        dz = t0 * d + t1 * s1 + t2 * s2
        dzb_ref[i] = dz.astype(BF16)
        rows_ref[i : i + 1, :] = jnp.sum(dz * zlow_ref[i], axis=0, keepdims=True)
        dlowd = dot_nt((dz * row_of(cst, SCALE + i)).astype(BF16), up_ref[i])
        grads.append(jnp.sum(dlowd * low_in, axis=0, keepdims=True))
        dlow = dlow + dlowd * row_of(cst, PICKED + i)
        inner = inner + dz * zraw_ref[i]
    for i in range(3):
        rows_ref[3 + i : 4 + i, :] = grads[i]
    rows_ref[6:7, :] = last_ref[0:1, :]
    rows_ref[7:8, :] = jnp.zeros((1, C), F32)
    inner = line(jnp.sum(inner + dlow * low_raw, axis=1, keepdims=True))
    low = dlow.astype(BF16)
    tail = tile_of(thirds(inner))
    for ref in (fa_ref, fb_ref):
        ref[512:768, :] = low
        ref[768:784, :] = tail
    for k, dst in ((3, None), (2, right_ref), (1, left_ref), (0, own_ref)):
        for r in range(4):
            at = ids[k][r]
            acc = dot_nt(dzb_ref[0], w_ref[0, at])
            acc = acc + dot_nt(dzb_ref[1], w_ref[1, at])
            acc = acc + dot_nt(dzb_ref[2], w_ref[2, at])
            part = acc.astype(BF16)
            if dst is None:
                half = fa_ref if r < 2 else fb_ref
                half[(r % 2) * 256 : (r % 2) * 256 + 256, :] = part
            else:
                dst[r * 256 : r * 256 + 256, :] = part


def merge_kernel(cut, low, right, left, ra, rb, right_out, left_out):
    right_out[0:512, :] = (right[0:512, :].astype(F32) + ra[0:512, :].astype(F32)).astype(BF16)
    right_out[512:1024, :] = right[512:1024, :]
    right_out[1024 : 1024 + cut, :] = ra[512 : 512 + cut, :]
    left_out[0:512, :] = left[0:512, :]
    left_out[512:1024, :] = (left[512:1024, :].astype(F32) + rb[0:512, :].astype(F32)).astype(BF16)
    left_out[1024 : 1024 + low - cut, :] = rb[512 + cut : 512 + low, :]


def low_total(fa, ra, rb, rm, lm, cut, low):
    parts = []
    for lo, hi, far in ((0, cut, rm[1024 : 1024 + cut, :]), (cut, low, lm[1024 : 1024 + low - cut, :])):
        v = far.astype(F32)
        for src in (fa, ra, rb):
            v = v + src[512 + lo : 512 + hi, :].astype(F32)
        parts.append(v)
    return jnp.concatenate(parts, 0)


def out_sum_kernel(
    own, rm, lm, fa, ra, rb, c0, c1, c2, c3, cst, near, far, gos_ref,
):
    low = low_total(fa, ra, rb, rm, lm, CUT, 256)
    lowd = (low * row_of(cst, PICKED + 3)).astype(BF16)
    gos_ref[4:8, :] = jnp.zeros((4, C), F32)
    for r, z in enumerate((c0, c1, c2, c3)):
        at = slice(r * 256, r * 256 + 256)
        olow = dot(lowd, z[256:512, :])
        scale = joined(z[512:528, :].astype(F32), 0)
        v = own[at, :].astype(F32) + rm[at, :].astype(F32) + lm[at, :].astype(F32) + olow * scale
        dst = near if r < 2 else far
        dst[(r % 2) * 256 : (r % 2) * 256 + 256, :] = v.astype(BF16)
        gos_ref[r : r + 1, :] = jnp.sum(z[:256, :].astype(F32) * olow, axis=0, keepdims=True)


def out_half_kernel(near, far, keep, send):
    keep[...] = near[0:256, :].astype(F32) + far[0:256, :].astype(F32)
    send[...] = (near[256:512, :].astype(F32) + far[256:512, :].astype(F32)).astype(BF16)


def in_sum_kernel(
    own, rm, lm, fa, ra, rb, z0, z1, z2, z3, rep, gos, o0, o1, o2, o3, keep,
):
    low = low_total(fa, ra, rb, rm, lm, CUT_T, LOW_T)
    dlow = low[:256].astype(BF16)
    inner = joined(low[256:], 0)
    grads = [rep[3 + i : 4 + i, :] for i in range(4)]
    keep[0:1, :] = inner
    for i in range(4):
        keep[1 + i : 2 + i, :] = grads[i]
    keep[5:6, :] = gos[0:1, :]
    keep[6:8, :] = jnp.zeros((2, C), F32)
    common = []
    for row in [inner] + grads:
        common = common + thirds(row)
    for r, (z, out) in enumerate(((z0, o0), (z1, o1), (z2, o2), (z3, o3))):
        at = slice(r * 256, r * 256 + 256)
        v = own[at, :].astype(F32) + rm[at, :].astype(F32) + lm[at, :].astype(F32)
        v = v + dot_nt(dlow, z[256:512, :])
        out[0:256, :] = v.astype(out.dtype)
        if r > 0:
            out[256:288, :] = tile_of(common + thirds(gos[r : r + 1, :]), 32)


def final_kernel(
    pick, o0, r1, r2, r3, keep, tok, cot, gain, rstd_ref, grad_ref, table_ref, gos_ref,
):
    dnorm = o0[...]
    rows = [keep[i : i + 1, :] for i in range(6)]
    for ref in (r1, r2, r3):
        dnorm = dnorm + ref[0:256, :].astype(F32)
        tail = ref[256:288, :].astype(F32)
        rows = [rows[i] + joined(tail, 3 * i) for i in range(6)]
    rstd = rstd_ref[...]
    inner = column(rows[0]) * (rstd * rstd * rstd / WIDTH)
    x = tok[...].astype(F32)
    grad = cot[...].astype(F32) + rstd * (gain[...].astype(F32) * dnorm) - x * inner
    grad_ref[...] = grad.astype(BF16)
    gos_ref[...] = rows[5]
    for g in range(4):
        out = jnp.zeros((1, RANK), F32)
        for i in range(4):
            chosen = jnp.full((1, RANK), pick[i], jnp.int32) == g
            out = out + jnp.where(chosen, rows[1 + i], 0.0)
        table_ref[g : g + 1, :] = out


VMEM = pl.BlockSpec(memory_space=pltpu.VMEM)
SMEM = pl.BlockSpec(memory_space=pltpu.SMEM)


def call(kernel, outs, args, scalars=False, scratch=(), flops=1 << 24, after=(), hold=()):
    specs = [VMEM] * len(args)
    if scalars:
        specs[0] = SMEM
    body = kernel
    if after or hold:
        n, m = len(args), len(after) + len(hold)

        def body(*refs):
            kernel(*refs[:n], *refs[n + m :])

        specs = specs + [VMEM] * len(hold) + [pl.BlockSpec(memory_space=pl.ANY)] * len(after)
        args = list(args) + list(hold) + list(after)
    outs = [jax.ShapeDtypeStruct(s, d) for s, d in outs]
    size = sum(v.size * v.dtype.itemsize for v in list(args) + outs)
    return pl.pallas_call(
        body,
        out_shape=outs,
        in_specs=specs,
        out_specs=[VMEM] * len(outs),
        scratch_shapes=list(scratch),
        compiler_params=pltpu.CompilerParams(vmem_limit_bytes=16 * 2**20),
        cost_estimate=pl.CostEstimate(flops=flops, bytes_accessed=size, transcendentals=0),
    )(*args)


def merge(cut, low, *args, after=()):
    def kernel(*refs):
        merge_kernel(cut, low, *refs)

    return call(kernel, [((1024 + cut, C), BF16), ((1024 + low - cut, C), BF16)], args, after=after)


def on_device(
    tokens,
    cotangent,
    norm_gain,
    in_weight,
    in_down,
    in_up,
    in_scale,
    scale_table,
    table_pick,
    short_taps,
    residue,
    decay,
    skip_gain,
    out_weight,
    out_down,
    out_up,
    out_scale,
):
    kap = residue * jnp.sqrt(-jnp.expm1(-2.0 * decay))
    weight = jnp.transpose(in_weight, (1, 0, 2)).reshape(3, 16, 256, C)
    up_in = jnp.transpose(in_up, (1, 0, 2))
    gain = norm_gain[None]
    (cst,) = call(
        const_kernel,
        [((24, C), F32)],
        [table_pick, kap[None], decay[None], skip_gain[None], in_scale, short_taps, scale_table],
        scalars=True,
        hold=[weight, up_in],
    )
    tz0 = jnp.concatenate([tokens, in_down, gain, jnp.zeros((15, C), BF16)], 0)
    tz = [tz0] + [across(tz0, "zh", r) for r in (1, 2, 3)]
    (cz0,) = call(
        cot_start_kernel, [((528, C), BF16)], [cotangent, out_up, out_scale[None], tz[2]]
    )
    cz = [cz0] + [across(cz0, "zh", r) for r in (1, 2, 3)]
    (pay,) = call(token_kernel, [((1296, C), BF16)], tz, after=[cst])
    tr, _ = ring_gather(pay, 656)
    (cpay,) = call(cot_kernel, [((1280, C), BF16)], cz)
    cr, far = ring_gather(cpay, 640)
    zraw, z, zlow, h, edge, low_raw, rstd = call(
        fwd_in_kernel,
        [((3, T, C), F32), ((3, T, C), BF16), ((3, T, C), F32), ((T, C), F32), ((16, C), F32),
         ((T, RANK), F32), ((T, 1), F32)],
        [*tr, weight, up_in, cst],
        after=[cpay],
        flops=2 * T * WIDTH * 3 * C,
    )
    edges = ctx_gather(edge)
    side = [((768, C), BF16)] * 2 + [((1024, C), BF16)] * 3
    gated, q, kf, vf, mix, nxt = call(
        fwd_out_kernel,
        [((T, C), BF16)] + [((T, C), F32)] * 4 + [((8, C), F32)],
        [*edges, z, h, cst],
        after=[far],
        scratch=[pltpu.VMEM((SLABS, 16, C), F32)],
    )
    fa, fb, right, left, own = call(
        part_kernel, side, [gated, out_down, out_weight], flops=2 * T * WIDTH * C
    )
    dg, gsum, gedge, last = call(
        bwd_in_kernel,
        [((T, C), F32), ((T, C), F32), ((8, C), F32), ((8, RANK), F32)],
        [*cr, out_weight, out_down, q, fa, cst],
        flops=2 * T * WIDTH * C,
    )
    ra, rb = shift(fa, "x", 1), shift(fb, "x", -1)
    right, left = merge(CUT, 256, right, left, ra, rb, after=[dg])
    rm, lm = shift(right, "x", 1), shift(left, "x", -1)
    half = [((512, C), BF16)] * 2
    near, far_out, gos = call(
        out_sum_kernel, half + [((8, C), F32)], [own, rm, lm, fa, ra, rb, *cz, cst]
    )
    keep, send = call(
        out_half_kernel, [((T, C), F32), ((T, C), BF16)], [near, across(far_out, "zh", 2)]
    )
    mixed = tokens.astype(F32) + keep + across(send, "zh", 1).astype(F32)
    mixed = mixed.astype(BF16)

    gedges = ctx_gather(gedge)
    side = [((784, C), BF16)] * 2 + [((1024, C), BF16)] * 3
    fa, fb, right, left, own, sums = call(
        bwd_out_kernel,
        side + [((8, C), F32)],
        [*gedges, dg, gsum, q, kf, vf, mix, nxt, cst, zraw, zlow, low_raw, rstd, last, up_in,
         weight],
        after=[near],
        scratch=[pltpu.VMEM((3, T, C), BF16), pltpu.VMEM((SLABS, 8, C), F32)],
        flops=2 * T * WIDTH * 3 * C,
    )
    ra, rb = shift(fa, "x", 1), shift(fb, "x", -1)
    right, left = merge(CUT_T, LOW_T, right, left, ra, rb)
    rm, lm = shift(right, "x", 1), shift(left, "x", -1)
    sums, gos = ctx_sum(stack(sums, gos))
    shared = sums + shift(sums, "x", 1) + shift(sums, "x", 2) + shift(sums, "x", 3)
    payload = [((T, C), F32)] + [((288, C), BF16)] * 3 + [((8, C), F32)]
    o0, o1, o2, o3, keep = call(
        in_sum_kernel, payload, [own, rm, lm, fa, ra, rb, *tz, shared, gos], after=[mixed]
    )
    got = [across(o, "zh", r) for r, o in ((1, o1), (2, o2), (3, o3))]
    grad_tokens, grad_table, grad_out_scale = call(
        final_kernel,
        [((T, C), BF16), ((4, RANK), F32), ((1, C), F32)],
        [table_pick, o0, *got, keep, tokens, cotangent, gain, rstd],
        scalars=True,
    )
    return (mixed, grad_tokens, grad_table, sums[:3], grad_out_scale[0])


def solution(mesh):
    fine = Mesh(mesh.devices.reshape(2, 4, 2, 4, 4), CTX + TP)
    return jax.shard_map(
        on_device,
        mesh=fine,
        in_specs=(
            P(CTX, TP),
            P(CTX, TP),
            P(TP),
            P(None, None, TP),
            P(TP, None),
            P(None, None, TP),
            P(None, TP),
            P(),
            P(),
            P(None, None, TP),
            P(TP),
            P(TP),
            P(TP),
            P(TP, None),
            P(TP, None),
            P(None, TP),
            P(TP),
        ),
        out_specs=(P(CTX, TP), P(CTX, TP), P(), P(None, TP), P(TP)),
        check_vma=False,
    )
```

```python
import jax
import jax.numpy as jnp
from jax import lax
from jax.experimental import pallas as pl
from jax.experimental.pallas import tpu as pltpu
from jax.sharding import Mesh, PartitionSpec as P

HIGH = lax.Precision.HIGHEST
CTX = ("zl", "y", "core")
TP = ("x", "zh")
F32 = jnp.float32
BF16 = jnp.bfloat16
T = 256
C = 256
RANK = 256
SLABS = 16
LOW_T = 272
CUT_T = 144
CUT = 128
WIDTH = 4096
KAP, DEC, SKIP, SCALE, TAPS, PICKED = 0, 1, 2, 3, 6, 15


def shift(v, axis, k):
    return lax.ppermute(v, axis, [(i, (i + k) % 4) for i in range(4)])


def swap(v, axis):
    return lax.ppermute(v, axis, [(0, 1), (1, 0)])


def stack(*parts):
    def kernel(*refs):
        for i, ref in enumerate(refs[:-1]):
            refs[-1][i] = ref[...]

    return call(kernel, [((len(parts),) + parts[0].shape, parts[0].dtype)], parts)[0]


def ctx_gather(v):
    first = stack(v, swap(v, "core"))
    v = stack(first, across(first, "y", 1))
    v = stack(v, across(v, "y", 2))
    return [v, swap(v, "zl")], first


def across(v, axis, bit):
    return lax.ppermute(v, axis, [(i, i ^ bit) for i in range(4)])


def ctx_spread(v):
    wide = jnp.broadcast_to(v[None], (SLABS,) + v.shape)
    return lax.all_to_all(wide, CTX, split_axis=0, concat_axis=0, tiled=True)


def place(scr, near, other):
    zl, y, core = (lax.axis_index(a) for a in CTX)
    for kz, src in enumerate((near, other)):
        for ky in range(4):
            for kc in range(2):
                slab = (1 - zl if kz else zl) * 8 + jnp.bitwise_xor(y, ky) * 2
                slab = slab + (1 - core if kc else core)
                scr[slab] = src[ky // 2, ky % 2, kc]


def position():
    zl, y, core = (lax.axis_index(a) for a in CTX)
    return zl * 8 + y * 2 + core


def block_ids():
    x, zh = lax.axis_index("x"), lax.axis_index("zh")
    xs = [x, lax.rem(x + 3, 4), lax.rem(x + 1, 4), lax.rem(x + 2, 4)]
    zs = [jnp.bitwise_xor(zh, r) for r in range(4)]
    return [[a * 4 + b for b in zs] for a in xs]


def x_gather(own):
    return [own, shift(own, "x", 1), shift(own, "x", -1), shift(own, "x", 2)]


def ring_gather(own, cut):
    left, right = shift(own, "x", 1), shift(own, "x", -1)
    rows = own.shape[0]

    def kernel(left_ref, right_ref, fa, fb):
        fa[...] = left_ref[0:cut, :]
        fb[...] = right_ref[cut:rows, :]

    shapes = [((cut, C), BF16), ((rows - cut, C), BF16)]
    fa, fb = call(kernel, shapes, [left, right])
    return [own, left, right, shift(fa, "x", 1), shift(fb, "x", -1)]


def x_scatter(right, left, far):
    return [shift(right, "x", 1), shift(left, "x", -1), shift(far, "x", 2)]


def as_pairs(quad, cut):
    return [(g.at[0:cut, :], g.at[cut:, :]) for g in quad]


def dot(a, b):
    return jnp.dot(a, b, preferred_element_type=F32)


def dot_nt(a, b):
    return lax.dot_general(a, b, (((1,), (1,)), ((), ())), preferred_element_type=F32)


def rnd(v):
    return v.astype(BF16).astype(F32)


def row_ids():
    return lax.broadcasted_iota(jnp.int32, (T, C), 0)


def column(row):
    square = (T, T)
    same = lax.broadcasted_iota(jnp.int32, square, 0) == lax.broadcasted_iota(jnp.int32, square, 1)
    return jnp.sum(jnp.where(same, row, 0.0), axis=1, keepdims=True)


def line(col):
    square = (T, T)
    same = lax.broadcasted_iota(jnp.int32, square, 0) == lax.broadcasted_iota(jnp.int32, square, 1)
    return jnp.sum(jnp.where(same, col, 0.0), axis=0, keepdims=True)


def thirds(row):
    hi = rnd(row)
    mid = rnd(row - hi)
    return [hi, mid, row - hi - mid]


def tile_of(rows, n=16):
    at = lax.broadcasted_iota(jnp.int32, (n, C), 0)
    out = jnp.zeros((n, C), F32)
    for i, row in enumerate(rows):
        out = jnp.where(at == i, row, out)
    return out.astype(BF16)


def joined(tile, i):
    return tile[i : i + 1] + tile[i + 1 : i + 2] + tile[i + 2 : i + 3]


def down(v, n, rows):
    return jnp.where(rows >= n, pltpu.roll(v, n, 0), 0.0)


def up(v, n, rows):
    return jnp.where(rows < T - n, pltpu.roll(v, T - n, 0), 0.0)


def scan_down(v, dec, rows):
    for k in range(8):
        n = 1 << k
        v = v + jnp.exp(-dec * n) * down(v, n, rows)
    return v


def scan_up(v, dec, rows):
    for k in range(8):
        n = 1 << k
        v = v + jnp.exp(-dec * n) * up(v, n, rows)
    return v


def row_of(ref, n):
    return ref[n : n + 1, :]


def blk(a_ref, b_ref, r, head):
    if r < 2:
        return a_ref[r * 256 : r * 256 + 256, :]
    at = head + (r - 2) * 256
    return b_ref[at : at + 256, :]


def put_blk(a_ref, b_ref, r, head, v):
    if r < 2:
        a_ref[r * 256 : r * 256 + 256, :] = v
    else:
        at = head + (r - 2) * 256
        b_ref[at : at + 256, :] = v


def low_sum(pairs, cut, low):
    out = []
    for part, size in ((0, cut), (1, low - cut)):
        at = 512 if part == 0 else 0
        v = 0.0
        for pair in pairs:
            v = v + pair[part][at : at + size, :].astype(F32)
        out.append(v)
    return jnp.concatenate(out, 0)


def const_kernel(pick, kap, dec, skip, scale, taps, table, cst):
    cst[0:1, :] = kap[...]
    cst[1:2, :] = dec[...]
    cst[2:3, :] = skip[...]
    cst[3:6, :] = scale[...]
    for i in range(3):
        for j in range(3):
            cst[TAPS + 3 * i + j : TAPS + 3 * i + j + 1, :] = taps[i, j : j + 1, :]
    for i in range(4):
        row = jnp.zeros((1, RANK), F32)
        for g in range(4):
            chosen = jnp.full((1, RANK), pick[i], jnp.int32) == g
            row = row + jnp.where(chosen, table[g : g + 1, :], 0.0)
        cst[PICKED + i : PICKED + i + 1, :] = row
    cst[19:24, :] = jnp.zeros((5, C), F32)


def cot_start_kernel(cot, upw, scale, after, pay):
    pay[0:256, :] = cot[...]
    pay[256:512, :] = upw[...]
    at = lax.broadcasted_iota(jnp.int32, (16, C), 0)
    rows = after[512:528, :].astype(F32)
    for i, row in enumerate(thirds(scale[...])):
        rows = jnp.where(at == i, row, rows)
    pay[512:528, :] = rows.astype(BF16)


def token_kernel(z0, z1, z2, z3, out):
    a_ref, b_ref = out.at[0:656, :], out.at[656:1296, :]
    low = jnp.zeros((T, RANK), F32)
    squares = jnp.zeros((T, 1), F32)
    for r, z in enumerate((z0, z1, z2, z3)):
        x = z[:256, :].astype(F32)
        gain = z[512:528, :].astype(F32)[:1]
        xg = (x * gain).astype(BF16)
        put_blk(a_ref, b_ref, r, 128, xg)
        low = low + dot(xg, z[256:512, :])
        squares = squares + jnp.sum(x * x, axis=1, keepdims=True)
    low = low.astype(BF16)
    a_ref[512:656, :] = low[:144]
    b_ref[0:112, :] = low[144:]
    b_ref[112:128, :] = tile_of(thirds(line(squares)))


def cot_kernel(z0, z1, z2, z3, out):
    a_ref, b_ref = out.at[0:640, :], out.at[640:1280, :]
    low = jnp.zeros((T, RANK), F32)
    for r, z in enumerate((z0, z1, z2, z3)):
        cot = z[:256, :]
        scale = joined(z[512:528, :].astype(F32), 0)
        put_blk(a_ref, b_ref, r, 128, cot)
        low = low + dot_nt((cot.astype(F32) * scale).astype(BF16), z[256:512, :])
    low = low.astype(BF16)
    a_ref[512:640, :] = low[:128]
    b_ref[0:128, :] = low[128:]


def fwd_in_kernel(
    g0, g1, g2, ga, gb, w_ref, up_ref, cst,
    zraw_ref, z_ref, zlow_ref, h_ref, edge_ref, low_ref, rstd_ref,
):
    rows = row_ids()
    ids = block_ids()
    pairs = as_pairs((g0, g1, g2), 656) + [(ga, gb)]
    total = low_sum(pairs, CUT_T, LOW_T)
    rstd = column(lax.rsqrt(joined(total[256:], 0) / WIDTH + 1e-06))
    rstd_ref[...] = rstd
    low_ref[...] = total[:256]
    low_in = low_ref[...] * rstd
    dec = row_of(cst, DEC)
    feat = []
    for i in range(3):
        acc = jnp.zeros((T, C), F32)
        for k, pair in enumerate(pairs):
            for r in range(4):
                acc = acc + dot(blk(*pair, r, 128), w_ref[i, ids[k][r]])
        zraw_ref[i] = acc
        zlow = dot((low_in * row_of(cst, PICKED + i)).astype(BF16), up_ref[i])
        zlow_ref[i] = zlow
        z = (acc * rstd + zlow * row_of(cst, SCALE + i)).astype(BF16)
        z_ref[i] = z
        z = z.astype(F32)
        edge_ref[1 + 4 * i : 3 + 4 * i, :] = z[:2]
        edge_ref[3 + 4 * i : 5 + 4 * i, :] = z[T - 2 :]
        if i > 0:
            f = row_of(cst, TAPS + 3 * i) * z
            for tap in (1, 2):
                f = f + row_of(cst, TAPS + 3 * i + tap) * down(z, tap, rows)
            feat.append(f)
    u = jnp.where(rows >= 2, rnd(feat[0] * feat[1]), 0.0)
    h = scan_down(row_of(cst, KAP) * u, dec, rows)
    h_ref[...] = h
    edge_ref[0:1, :] = h[T - 1 :]
    edge_ref[13:16, :] = jnp.zeros((3, C), F32)


def fwd_out_kernel(
    near, other, z_ref, h_ref, cst, down_ref,
    gated_ref, low_ref, q_ref, k_ref, v_ref, mix_ref, next_ref, edges_ref,
):
    me = position()
    place(edges_ref, near, other)
    rows = row_ids()
    dec = row_of(cst, DEC)
    kap = row_of(cst, KAP)
    skip = row_of(cst, SKIP)
    slab = lax.broadcasted_iota(jnp.int32, (SLABS, C), 0)

    def edge(r):
        return edges_ref[:, r, :]

    def prev(v):
        return jnp.where(slab >= 1, pltpu.roll(v, 1, 0), 0.0)

    def own(v):
        return jnp.sum(jnp.where(slab == me, v, 0.0), axis=0, keepdims=True)

    def following(v):
        return jnp.sum(jnp.where(slab == me + 1, v, 0.0), axis=0, keepdims=True)

    first0, first1, full = [], [], []
    for i in range(3):
        t0, t1, t2 = (row_of(cst, TAPS + 3 * i + n) for n in range(3))
        a0, a1 = edge(1 + 4 * i), edge(2 + 4 * i)
        b0, b1 = prev(edge(3 + 4 * i)), prev(edge(4 + 4 * i))
        first0.append(t0 * a0 + t1 * b1 + t2 * b0)
        first1.append(t0 * a1 + t1 * a0 + t2 * b1)
        p0, p1 = own(b0), own(b1)
        z = z_ref[i].astype(F32)
        s1 = jnp.where(rows == 0, p1, pltpu.roll(z, 1, 0))
        s2 = jnp.where(rows == 0, p0, jnp.where(rows == 1, p1, pltpu.roll(z, 2, 0)))
        full.append(t0 * z + t1 * s1 + t2 * s2)
    u0 = rnd(first0[1] * first0[2])
    u1 = rnd(first1[1] * first1[2])
    total = edge(0) + kap * (jnp.exp(-dec * (T - 1)) * u0 + jnp.exp(-dec * (T - 2)) * u1)
    ahead = (me - 1 - slab).astype(F32)
    weight = jnp.exp(-dec * (T * jnp.maximum(ahead, 0.0)))
    carry = jnp.sum(jnp.where(slab < me, weight * total, 0.0), axis=0, keepdims=True)
    carry_next = jnp.exp(-dec * T) * carry + own(total)
    one = jnp.exp(-dec)
    power = jnp.exp(-dec * rows.astype(F32))
    bump = jnp.where(rows >= 1, kap * own(u1) * jnp.exp(dec), 0.0)
    h = h_ref[...] + power * (one * carry + kap * own(u0) + bump)
    q, kf, vf = full
    mix = rnd(h) + skip * rnd(kf * vf)
    gated = (q * mix).astype(BF16)
    gated_ref[...] = gated
    low_ref[...] = dot(gated, down_ref[...]).astype(BF16)
    q_ref[...] = q
    k_ref[...] = kf
    v_ref[...] = vf
    mix_ref[...] = mix
    n0 = following(u0)
    n1 = following(u1)
    h0 = one * carry_next + kap * n0
    h1 = one * h0 + kap * n1
    next_ref[0:1, :] = rnd(h0) + skip * n0
    next_ref[1:2, :] = rnd(h1) + skip * n1
    for i in range(3):
        next_ref[2 + 2 * i : 3 + 2 * i, :] = following(first0[i])
        next_ref[3 + 2 * i : 4 + 2 * i, :] = following(first1[i])


def part_kernel(gated_ref, low_ref, ow_ref, right_ref, left_ref, far_ref, own_ref):
    ids = block_ids()
    gated = gated_ref[...]
    for k, dst in ((3, far_ref), (2, right_ref), (1, left_ref), (0, own_ref)):
        if k > 0:
            dst[1024:1280, :] = low_ref[...]
        for r in range(4):
            cols = pl.ds(pl.multiple_of(ids[k][r] * 256, 256), 256)
            dst[r * 256 : r * 256 + 256, :] = dot(gated, ow_ref[:, cols]).astype(BF16)


def bwd_in_kernel(
    g0, g1, g2, g3, ow_ref, down_ref, q_ref, low_out, cst,
    dg_ref, gsum_ref, edge_ref, last_ref,
):
    rows = row_ids()
    dec = row_of(cst, DEC)
    ids = block_ids()
    pairs = as_pairs((g0, g1, g2, g3), 640)
    dlowd = low_sum(pairs, CUT, 256)
    last = jnp.sum(dlowd * low_out[...].astype(F32), axis=0, keepdims=True)
    last_ref[...] = jnp.broadcast_to(last, (8, RANK))
    dg = dot_nt((dlowd * row_of(cst, PICKED + 3)).astype(BF16), down_ref[...])
    for k, pair in enumerate(pairs):
        for r in range(4):
            cols = pl.ds(pl.multiple_of(ids[k][r] * 256, 256), 256)
            dg = dg + dot_nt(blk(*pair, r, 128), ow_ref[:, cols])
    dg_ref[...] = dg
    g = scan_up(row_of(cst, KAP) * rnd(dg * q_ref[...]), dec, rows)
    gsum_ref[...] = g
    edge_ref[0:2, :] = g[:2]
    edge_ref[2:4, :] = dg[:2]
    edge_ref[4:8, :] = jnp.zeros((4, C), F32)


def bwd_out_kernel(
    near, other, dg_ref, g_ref, q_ref, k_ref, v_ref, mix_ref, next_ref, cst, zraw_ref,
    zlow_ref, low_ref, rstd_ref, last_ref, up_ref, w_ref,
    right_ref, left_ref, far_ref, own_ref, rows_ref, dzb_ref, edges_ref,
):
    me = position()
    ids = block_ids()
    place(edges_ref, near, other)
    rows = row_ids()
    dec = row_of(cst, DEC)
    skip = row_of(cst, SKIP)
    slab = lax.broadcasted_iota(jnp.int32, (SLABS, C), 0)

    def following(v):
        return jnp.sum(jnp.where(slab == me + 1, v, 0.0), axis=0, keepdims=True)

    head = edges_ref[:, 0, :]
    ahead = (slab - me - 1).astype(F32)
    weight = jnp.exp(-dec * (T * jnp.maximum(ahead, 0.0)))
    carry = jnp.sum(jnp.where(slab > me, weight * head, 0.0), axis=0, keepdims=True)
    weight = jnp.exp(-dec * (T * jnp.maximum(ahead - 1.0, 0.0)))
    carry_next = jnp.sum(jnp.where(slab > me + 1, weight * head, 0.0), axis=0, keepdims=True)
    g = g_ref[...] + jnp.exp(-dec * (T - rows).astype(F32)) * carry
    dg = dg_ref[...]
    q, kf, vf = q_ref[...], k_ref[...], v_ref[...]
    dprod = rnd(g) + skip * (dg * q)
    dfeat = (dg * mix_ref[...], dprod * vf, dprod * kf)
    dg0 = following(edges_ref[:, 2, :])
    dg1 = following(edges_ref[:, 3, :])
    g1 = following(edges_ref[:, 1, :]) + jnp.exp(-dec * (T - 1)) * carry_next
    nxt = [row_of(next_ref, n) for n in range(8)]
    dp0 = rnd(carry) + skip * (dg0 * nxt[2])
    dp1 = rnd(g1) + skip * (dg1 * nxt[3])
    inside = jnp.full((1, C), me, jnp.int32) < SLABS - 1
    after0 = [jnp.where(inside, v, 0.0) for v in (dg0 * nxt[0], dp0 * nxt[6], dp0 * nxt[4])]
    after1 = [jnp.where(inside, v, 0.0) for v in (dg1 * nxt[1], dp1 * nxt[7], dp1 * nxt[5])]
    low_raw = low_ref[...]
    low_in = low_raw * rstd_ref[...]
    dlow = jnp.zeros((T, RANK), F32)
    inner = jnp.zeros((T, C), F32)
    grads = []
    for i in range(3):
        t0, t1, t2 = (row_of(cst, TAPS + 3 * i + n) for n in range(3))
        d = dfeat[i]
        s1 = jnp.where(rows == T - 1, after0[i], pltpu.roll(d, T - 1, 0))
        s2 = jnp.where(
            rows == T - 2, after0[i], jnp.where(rows == T - 1, after1[i], pltpu.roll(d, T - 2, 0))
        )
        dz = t0 * d + t1 * s1 + t2 * s2
        dzb_ref[i] = dz.astype(BF16)
        rows_ref[i : i + 1, :] = jnp.sum(dz * zlow_ref[i], axis=0, keepdims=True)
        dlowd = dot_nt((dz * row_of(cst, SCALE + i)).astype(BF16), up_ref[i])
        grads.append(jnp.sum(dlowd * low_in, axis=0, keepdims=True))
        dlow = dlow + dlowd * row_of(cst, PICKED + i)
        inner = inner + dz * zraw_ref[i]
    rows_ref[3:8, :] = jnp.zeros((5, C), F32)
    inner = line(jnp.sum(inner + dlow * low_raw, axis=1, keepdims=True))
    low = dlow.astype(BF16)
    tail = thirds(inner)
    for row in grads + [last_ref[0:1, :]]:
        tail = tail + thirds(row)
    tail = tile_of(tail)
    for k, dst in ((3, far_ref), (2, right_ref), (1, left_ref), (0, own_ref)):
        dst[1024:1280, :] = low
        dst[1280:1296, :] = tail
        for r in range(4):
            at = ids[k][r]
            acc = dot_nt(dzb_ref[0], w_ref[0, at])
            acc = acc + dot_nt(dzb_ref[1], w_ref[1, at])
            acc = acc + dot_nt(dzb_ref[2], w_ref[2, at])
            dst[r * 256 : r * 256 + 256, :] = acc.astype(BF16)


def total_of(parts, lo, hi):
    out = parts[0][lo:hi, :].astype(F32)
    for part in parts[1:]:
        out = out + part[lo:hi, :].astype(F32)
    return out


def out_sum_kernel(
    own, low_ref, rm, lm, fm, c0, c1, c2, c3, cst, near, far, gos_ref,
):
    parts = (own, rm, lm, fm)
    low = low_ref[...].astype(F32) + total_of(parts[1:], 1024, 1280)
    lowd = (low * row_of(cst, PICKED + 3)).astype(BF16)
    gos_ref[4:8, :] = jnp.zeros((4, C), F32)
    for r, z in enumerate((c0, c1, c2, c3)):
        olow = dot(lowd, z[256:512, :])
        scale = joined(z[512:528, :].astype(F32), 0)
        v = total_of(parts, r * 256, r * 256 + 256) + olow * scale
        dst = near if r < 2 else far
        dst[(r % 2) * 256 : (r % 2) * 256 + 256, :] = v.astype(BF16)
        gos_ref[r : r + 1, :] = jnp.sum(z[:256, :].astype(F32) * olow, axis=0, keepdims=True)


def out_half_kernel(near, far, keep, send):
    keep[...] = near[0:256, :].astype(F32) + far[0:256, :].astype(F32)
    send[...] = (near[256:512, :].astype(F32) + far[256:512, :].astype(F32)).astype(BF16)


def in_sum_kernel(
    own, rm, lm, fm, z0, z1, z2, z3, gos, o0, o1, o2, o3, keep,
):
    parts = (own, rm, lm, fm)
    low = total_of(parts, 1024, 1296)
    dlow = low[:256].astype(BF16)
    inner = joined(low[256:], 0)
    grads = [joined(low[256:], 3 + 3 * i) for i in range(4)]
    keep[0:1, :] = inner
    for i in range(4):
        keep[1 + i : 2 + i, :] = grads[i]
    keep[5:6, :] = gos[0:1, :]
    keep[6:8, :] = jnp.zeros((2, C), F32)
    common = []
    for row in [inner] + grads:
        common = common + thirds(row)
    for r, (z, out) in enumerate(((z0, o0), (z1, o1), (z2, o2), (z3, o3))):
        at = slice(r * 256, r * 256 + 256)
        v = total_of(parts, r * 256, r * 256 + 256)
        v = v + dot_nt(dlow, z[256:512, :])
        out[0:256, :] = v.astype(out.dtype)
        if r > 0:
            out[256:288, :] = tile_of(common + thirds(gos[r : r + 1, :]), 32)


def final_kernel(
    o0, r1, r2, r3, keep, sums, tok, cot, gain, rstd_ref, grad_ref, rows_ref,
):
    dnorm = o0[...]
    rows = [keep[i : i + 1, :] for i in range(6)]
    for ref in (r1, r2, r3):
        dnorm = dnorm + ref[0:256, :].astype(F32)
        tail = ref[256:288, :].astype(F32)
        rows = [rows[i] + joined(tail, 3 * i) for i in range(6)]
    rstd = rstd_ref[...]
    inner = column(rows[0]) * (rstd * rstd * rstd / WIDTH)
    x = tok[...].astype(F32)
    grad = cot[...].astype(F32) + rstd * (gain[...].astype(F32) * dnorm) - x * inner
    grad_ref[...] = grad.astype(BF16)
    rows_ref[0:3, :] = sums[0:3, :]
    rows_ref[3:4, :] = rows[5]
    for i in range(4):
        rows_ref[4 + i : 5 + i, :] = rows[1 + i]


def table_kernel(pick, rep, table_ref, gis_ref, gos_ref):
    rows = rep[0]
    for i in range(1, SLABS):
        rows = rows + rep[i]
    gis_ref[...] = rows[0:3]
    gos_ref[...] = rows[3:4]
    for g in range(4):
        out = jnp.zeros((1, RANK), F32)
        for i in range(4):
            chosen = jnp.full((1, RANK), pick[i], jnp.int32) == g
            out = out + jnp.where(chosen, rows[4 + i : 5 + i], 0.0)
        table_ref[g : g + 1, :] = out


VMEM = pl.BlockSpec(memory_space=pltpu.VMEM)
SMEM = pl.BlockSpec(memory_space=pltpu.SMEM)


def call(kernel, outs, args, scalars=False, scratch=(), flops=1 << 24, after=(), hold=()):
    specs = [VMEM] * len(args)
    if scalars:
        specs[0] = SMEM
    body = kernel
    if after or hold:
        n, m = len(args), len(after) + len(hold)

        def body(*refs):
            kernel(*refs[:n], *refs[n + m :])

        specs = specs + [VMEM] * len(hold) + [pl.BlockSpec(memory_space=pl.ANY)] * len(after)
        args = list(args) + list(hold) + list(after)
    outs = [jax.ShapeDtypeStruct(s, d) for s, d in outs]
    size = sum(v.size * v.dtype.itemsize for v in list(args) + outs)
    return pl.pallas_call(
        body,
        out_shape=outs,
        in_specs=specs,
        out_specs=[VMEM] * len(outs),
        scratch_shapes=list(scratch),
        compiler_params=pltpu.CompilerParams(vmem_limit_bytes=16 * 2**20),
        cost_estimate=pl.CostEstimate(flops=flops, bytes_accessed=size, transcendentals=0),
    )(*args)


def on_device(
    tokens,
    cotangent,
    norm_gain,
    in_weight,
    in_down,
    in_up,
    in_scale,
    scale_table,
    table_pick,
    short_taps,
    residue,
    decay,
    skip_gain,
    out_weight,
    out_down,
    out_up,
    out_scale,
):
    kap = residue * jnp.sqrt(-jnp.expm1(-2.0 * decay))
    weight = jnp.transpose(in_weight, (1, 0, 2)).reshape(3, 16, 256, C)
    up_in = jnp.transpose(in_up, (1, 0, 2))
    gain = norm_gain[None]
    (cst,) = call(
        const_kernel,
        [((24, C), F32)],
        [table_pick, kap[None], decay[None], skip_gain[None], in_scale, short_taps, scale_table],
        scalars=True,
        hold=[weight, up_in],
    )
    tz0 = jnp.concatenate([tokens, in_down, gain, jnp.zeros((15, C), BF16)], 0)
    tz = [tz0] + [across(tz0, "zh", r) for r in (1, 2, 3)]
    (cz0,) = call(
        cot_start_kernel, [((528, C), BF16)], [cotangent, out_up, out_scale[None], tz[2]]
    )
    cz = [cz0] + [across(cz0, "zh", r) for r in (1, 2, 3)]
    (pay,) = call(token_kernel, [((1296, C), BF16)], tz, after=[cst])
    tr = ring_gather(pay, 656)
    (cpay,) = call(cot_kernel, [((1280, C), BF16)], cz)
    cr = x_gather(cpay)
    zraw, z, zlow, h, edge, low_raw, rstd = call(
        fwd_in_kernel,
        [((3, T, C), F32), ((3, T, C), BF16), ((3, T, C), F32), ((T, C), F32), ((16, C), F32),
         ((T, RANK), F32), ((T, 1), F32)],
        [*tr, weight, up_in, cst],
        after=[cpay],
        flops=2 * T * WIDTH * 3 * C,
    )
    edges, _ = ctx_gather(edge)
    gated, low_out, q, kf, vf, mix, nxt = call(
        fwd_out_kernel,
        [((T, C), BF16)] * 2 + [((T, C), F32)] * 4 + [((8, C), F32)],
        [*edges, z, h, cst, out_down],
        scratch=[pltpu.VMEM((SLABS, 16, C), F32)],
    )
    *out, own_out = call(
        part_kernel,
        [((1280, C), BF16)] * 3 + [((1024, C), BF16)],
        [gated, low_out, out_weight],
        flops=2 * T * WIDTH * C,
    )
    got_out = x_scatter(*out)
    dg, gsum, gedge, last = call(
        bwd_in_kernel,
        [((T, C), F32), ((T, C), F32), ((8, C), F32), ((8, RANK), F32)],
        [*cr, out_weight, out_down, q, low_out, cst],
        after=[own_out],
        flops=2 * T * WIDTH * C,
    )
    gedges, _ = ctx_gather(gedge)
    *out, own, sums = call(
        bwd_out_kernel,
        [((1296, C), BF16)] * 4 + [((8, C), F32)],
        [*gedges, dg, gsum, q, kf, vf, mix, nxt, cst, zraw, zlow, low_raw, rstd, last, up_in,
         weight],
        scratch=[pltpu.VMEM((3, T, C), BF16), pltpu.VMEM((SLABS, 8, C), F32)],
        flops=2 * T * WIDTH * 3 * C,
    )
    got = x_scatter(*out)
    half = [((512, C), BF16)] * 2
    near, far_out, gos = call(
        out_sum_kernel, half + [((8, C), F32)], [own_out, low_out, *got_out, *cz, cst], after=[sums]
    )
    keep, send = call(
        out_half_kernel, [((T, C), F32), ((T, C), BF16)], [near, across(far_out, "zh", 2)]
    )
    mixed = tokens.astype(F32) + keep + across(send, "zh", 1).astype(F32)
    mixed = mixed.astype(BF16)

    payload = [((T, C), F32)] + [((288, C), BF16)] * 3 + [((8, C), F32)]
    o0, o1, o2, o3, inner = call(
        in_sum_kernel, payload, [own, *got, *tz, gos], after=[mixed]
    )
    got = [across(o, "zh", r) for r, o in ((1, o1), (2, o2), (3, o3))]
    grad_tokens, rows = call(
        final_kernel,
        [((T, C), BF16), ((8, C), F32)],
        [o0, *got, inner, sums, tokens, cotangent, gain, rstd],
    )
    grad_table, grad_in_scale, grad_out_scale = call(
        table_kernel,
        [((4, RANK), F32), ((3, C), F32), ((1, C), F32)],
        [table_pick, ctx_spread(rows)],
        scalars=True,
    )
    return (mixed, grad_tokens, grad_table, grad_in_scale, grad_out_scale[0])


def solution(mesh):
    fine = Mesh(mesh.devices.reshape(2, 4, 2, 4, 4), CTX + TP)
    return jax.shard_map(
        on_device,
        mesh=fine,
        in_specs=(
            P(CTX, TP),
            P(CTX, TP),
            P(TP),
            P(None, None, TP),
            P(TP, None),
            P(None, None, TP),
            P(None, TP),
            P(),
            P(),
            P(None, None, TP),
            P(TP),
            P(TP),
            P(TP),
            P(TP, None),
            P(TP, None),
            P(None, TP),
            P(TP),
        ),
        out_specs=(P(CTX, TP), P(CTX, TP), P(), P(None, TP), P(TP)),
        check_vma=False,
    )
```

```python
import jax
import jax.numpy as jnp
from jax import lax
from jax.experimental import pallas as pl
from jax.experimental.pallas import tpu as pltpu
from jax.sharding import Mesh, PartitionSpec as P

HIGH = lax.Precision.HIGHEST
CTX = ("zl", "y", "core")
TP = ("x", "zh")
F32 = jnp.float32
BF16 = jnp.bfloat16
T = 256
C = 256
RANK = 256
SLABS = 16
LOW_T = 272
CUT_T = 144
CUT = 128
WIDTH = 4096
KAP, DEC, SKIP, SCALE, TAPS, PICKED = 0, 1, 2, 3, 6, 15


def shift(v, axis, k):
    return lax.ppermute(v, axis, [(i, (i + k) % 4) for i in range(4)])


def swap(v, axis):
    return lax.ppermute(v, axis, [(0, 1), (1, 0)])


def stack(*parts):
    def kernel(*refs):
        for i, ref in enumerate(refs[:-1]):
            refs[-1][i] = ref[...]

    return call(kernel, [((len(parts),) + parts[0].shape, parts[0].dtype)], parts)[0]


def ctx_gather(v):
    first = stack(v, swap(v, "core"))
    v = stack(first, across(first, "y", 1))
    v = stack(v, across(v, "y", 2))
    return [v, swap(v, "zl")], first


def across(v, axis, bit):
    return lax.ppermute(v, axis, [(i, i ^ bit) for i in range(4)])


def ctx_spread(v):
    wide = jnp.broadcast_to(v[None], (SLABS,) + v.shape)
    return lax.all_to_all(wide, CTX, split_axis=0, concat_axis=0, tiled=True)


def place(scr, near, other):
    zl, y, core = (lax.axis_index(a) for a in CTX)
    for kz, src in enumerate((near, other)):
        for ky in range(4):
            for kc in range(2):
                slab = (1 - zl if kz else zl) * 8 + jnp.bitwise_xor(y, ky) * 2
                slab = slab + (1 - core if kc else core)
                scr[slab] = src[ky // 2, ky % 2, kc]


def position():
    zl, y, core = (lax.axis_index(a) for a in CTX)
    return zl * 8 + y * 2 + core


def block_ids():
    x, zh = lax.axis_index("x"), lax.axis_index("zh")
    xs = [x, lax.rem(x + 3, 4), lax.rem(x + 1, 4), lax.rem(x + 2, 4)]
    zs = [jnp.bitwise_xor(zh, r) for r in range(4)]
    return [[a * 4 + b for b in zs] for a in xs]


def x_gather(own):
    return [own, shift(own, "x", 1), shift(own, "x", -1), shift(own, "x", 2)]


def ring_gather(own, cut):
    left, right = shift(own, "x", 1), shift(own, "x", -1)
    rows = own.shape[0]

    def kernel(left_ref, right_ref, fa, fb):
        fa[...] = left_ref[0:cut, :]
        fb[...] = right_ref[cut:rows, :]

    shapes = [((cut, C), BF16), ((rows - cut, C), BF16)]
    fa, fb = call(kernel, shapes, [left, right])
    return [own, left, right, shift(fa, "x", 1), shift(fb, "x", -1)], fa


def x_scatter(right, left, far):
    return [shift(right, "x", 1), shift(left, "x", -1), shift(far, "x", 2)]


def as_pairs(quad, cut):
    return [(g.at[0:cut, :], g.at[cut:, :]) for g in quad]


def dot(a, b):
    return jnp.dot(a, b, preferred_element_type=F32)


def dot_nt(a, b):
    return lax.dot_general(a, b, (((1,), (1,)), ((), ())), preferred_element_type=F32)


def rnd(v):
    return v.astype(BF16).astype(F32)


def row_ids():
    return lax.broadcasted_iota(jnp.int32, (T, C), 0)


def column(row):
    square = (T, T)
    same = lax.broadcasted_iota(jnp.int32, square, 0) == lax.broadcasted_iota(jnp.int32, square, 1)
    return jnp.sum(jnp.where(same, row, 0.0), axis=1, keepdims=True)


def line(col):
    square = (T, T)
    same = lax.broadcasted_iota(jnp.int32, square, 0) == lax.broadcasted_iota(jnp.int32, square, 1)
    return jnp.sum(jnp.where(same, col, 0.0), axis=0, keepdims=True)


def thirds(row):
    hi = rnd(row)
    mid = rnd(row - hi)
    return [hi, mid, row - hi - mid]


def tile_of(rows, n=16):
    at = lax.broadcasted_iota(jnp.int32, (n, C), 0)
    out = jnp.zeros((n, C), F32)
    for i, row in enumerate(rows):
        out = jnp.where(at == i, row, out)
    return out.astype(BF16)


def joined(tile, i):
    return tile[i : i + 1] + tile[i + 1 : i + 2] + tile[i + 2 : i + 3]


def down(v, n, rows):
    return jnp.where(rows >= n, pltpu.roll(v, n, 0), 0.0)


def up(v, n, rows):
    return jnp.where(rows < T - n, pltpu.roll(v, T - n, 0), 0.0)


def scan_down(v, dec, rows):
    for k in range(8):
        n = 1 << k
        v = v + jnp.exp(-dec * n) * down(v, n, rows)
    return v


def scan_up(v, dec, rows):
    for k in range(8):
        n = 1 << k
        v = v + jnp.exp(-dec * n) * up(v, n, rows)
    return v


def row_of(ref, n):
    return ref[n : n + 1, :]


def blk(a_ref, b_ref, r, head):
    if r < 2:
        return a_ref[r * 256 : r * 256 + 256, :]
    at = head + (r - 2) * 256
    return b_ref[at : at + 256, :]


def put_blk(a_ref, b_ref, r, head, v):
    if r < 2:
        a_ref[r * 256 : r * 256 + 256, :] = v
    else:
        at = head + (r - 2) * 256
        b_ref[at : at + 256, :] = v


def low_sum(pairs, cut, low):
    out = []
    for part, size in ((0, cut), (1, low - cut)):
        at = 512 if part == 0 else 0
        v = 0.0
        for pair in pairs:
            v = v + pair[part][at : at + size, :].astype(F32)
        out.append(v)
    return jnp.concatenate(out, 0)


def const_kernel(pick, kap, dec, skip, scale, taps, table, cst):
    cst[0:1, :] = kap[...]
    cst[1:2, :] = dec[...]
    cst[2:3, :] = skip[...]
    cst[3:6, :] = scale[...]
    for i in range(3):
        for j in range(3):
            cst[TAPS + 3 * i + j : TAPS + 3 * i + j + 1, :] = taps[i, j : j + 1, :]
    for i in range(4):
        row = jnp.zeros((1, RANK), F32)
        for g in range(4):
            chosen = jnp.full((1, RANK), pick[i], jnp.int32) == g
            row = row + jnp.where(chosen, table[g : g + 1, :], 0.0)
        cst[PICKED + i : PICKED + i + 1, :] = row
    cst[19:24, :] = jnp.zeros((5, C), F32)


def cot_start_kernel(cot, upw, scale, after, pay):
    core = lax.axis_index("core")
    pay[0:256, :] = cot[...]
    pay[256:384, :] = upw[pl.ds(pl.multiple_of(core * 128, 128), 128), :]
    at = lax.broadcasted_iota(jnp.int32, (16, C), 0)
    rows = after[384:400, :].astype(F32)
    for i, row in enumerate(thirds(scale[...])):
        rows = jnp.where(at == i, row, rows)
    pay[384:400, :] = rows.astype(BF16)


def halves_kernel(z1, z2, z3, out):
    for i, z in enumerate((z1, z2, z3)):
        out[i * 128 : i * 128 + 128, :] = z[256:384, :]


def join_halves(zs, other, own, whole):
    core = lax.axis_index("core")
    whole[0:256, :] = own[...]
    for r in (1, 2, 3):
        mine = pl.ds(pl.multiple_of(r * 256 + core * 128, 128), 128)
        rest = pl.ds(pl.multiple_of(r * 256 + 128 - core * 128, 128), 128)
        whole[mine, :] = zs[r][256:384, :]
        whole[rest, :] = other[r * 128 - 128 : r * 128, :]


def token_kernel(z0, z1, z2, z3, other, dn, out, whole):
    a_ref, b_ref = out.at[0:656, :], out.at[656:1296, :]
    zs = (z0, z1, z2, z3)
    join_halves(zs, other, dn, whole)
    low = jnp.zeros((T, RANK), F32)
    squares = jnp.zeros((T, 1), F32)
    for r, z in enumerate(zs):
        x = z[:256, :].astype(F32)
        gain = z[384:400, :].astype(F32)[:1]
        xg = (x * gain).astype(BF16)
        put_blk(a_ref, b_ref, r, 128, xg)
        low = low + dot(xg, whole[r * 256 : r * 256 + 256, :])
        squares = squares + jnp.sum(x * x, axis=1, keepdims=True)
    low = low.astype(BF16)
    a_ref[512:656, :] = low[:144]
    b_ref[0:112, :] = low[144:]
    b_ref[112:128, :] = tile_of(thirds(line(squares)))


def cot_kernel(z0, z1, z2, z3, other, upw, out, whole):
    a_ref, b_ref = out.at[0:640, :], out.at[640:1280, :]
    zs = (z0, z1, z2, z3)
    join_halves(zs, other, upw, whole)
    low = jnp.zeros((T, RANK), F32)
    for r, z in enumerate(zs):
        cot = z[:256, :]
        scale = joined(z[384:400, :].astype(F32), 0)
        put_blk(a_ref, b_ref, r, 128, cot)
        low = low + dot_nt(
            (cot.astype(F32) * scale).astype(BF16), whole[r * 256 : r * 256 + 256, :]
        )
    low = low.astype(BF16)
    a_ref[512:640, :] = low[:128]
    b_ref[0:128, :] = low[128:]


def fwd_in_kernel(
    g0, g1, g2, ga, gb, w_ref, up_ref, cst,
    zraw_ref, z_ref, zlow_ref, h_ref, edge_ref, low_ref, rstd_ref,
):
    rows = row_ids()
    ids = block_ids()
    pairs = as_pairs((g0, g1, g2), 656) + [(ga, gb)]
    total = low_sum(pairs, CUT_T, LOW_T)
    rstd = column(lax.rsqrt(joined(total[256:], 0) / WIDTH + 1e-06))
    rstd_ref[...] = rstd
    low_ref[...] = total[:256]
    low_in = low_ref[...] * rstd
    dec = row_of(cst, DEC)
    feat = []
    for i in range(3):
        acc = jnp.zeros((T, C), F32)
        for k, pair in enumerate(pairs):
            for r in range(4):
                acc = acc + dot(blk(*pair, r, 128), w_ref[i, ids[k][r]])
        zraw_ref[i] = acc
        zlow = dot((low_in * row_of(cst, PICKED + i)).astype(BF16), up_ref[i])
        zlow_ref[i] = zlow
        z = (acc * rstd + zlow * row_of(cst, SCALE + i)).astype(BF16)
        z_ref[i] = z
        z = z.astype(F32)
        edge_ref[1 + 4 * i : 3 + 4 * i, :] = z[:2]
        edge_ref[3 + 4 * i : 5 + 4 * i, :] = z[T - 2 :]
        if i > 0:
            f = row_of(cst, TAPS + 3 * i) * z
            for tap in (1, 2):
                f = f + row_of(cst, TAPS + 3 * i + tap) * down(z, tap, rows)
            feat.append(f)
    u = jnp.where(rows >= 2, rnd(feat[0] * feat[1]), 0.0)
    h = scan_down(row_of(cst, KAP) * u, dec, rows)
    h_ref[...] = h
    edge_ref[0:1, :] = h[T - 1 :]
    edge_ref[13:16, :] = jnp.zeros((3, C), F32)


def fwd_out_kernel(
    near, other, z_ref, h_ref, cst, down_ref,
    gated_ref, low_ref, q_ref, k_ref, v_ref, mix_ref, next_ref, edges_ref,
):
    me = position()
    place(edges_ref, near, other)
    rows = row_ids()
    dec = row_of(cst, DEC)
    kap = row_of(cst, KAP)
    skip = row_of(cst, SKIP)
    slab = lax.broadcasted_iota(jnp.int32, (SLABS, C), 0)

    def edge(r):
        return edges_ref[:, r, :]

    def prev(v):
        return jnp.where(slab >= 1, pltpu.roll(v, 1, 0), 0.0)

    def own(v):
        return jnp.sum(jnp.where(slab == me, v, 0.0), axis=0, keepdims=True)

    def following(v):
        return jnp.sum(jnp.where(slab == me + 1, v, 0.0), axis=0, keepdims=True)

    first0, first1, full = [], [], []
    for i in range(3):
        t0, t1, t2 = (row_of(cst, TAPS + 3 * i + n) for n in range(3))
        a0, a1 = edge(1 + 4 * i), edge(2 + 4 * i)
        b0, b1 = prev(edge(3 + 4 * i)), prev(edge(4 + 4 * i))
        first0.append(t0 * a0 + t1 * b1 + t2 * b0)
        first1.append(t0 * a1 + t1 * a0 + t2 * b1)
        p0, p1 = own(b0), own(b1)
        z = z_ref[i].astype(F32)
        s1 = jnp.where(rows == 0, p1, pltpu.roll(z, 1, 0))
        s2 = jnp.where(rows == 0, p0, jnp.where(rows == 1, p1, pltpu.roll(z, 2, 0)))
        full.append(t0 * z + t1 * s1 + t2 * s2)
    u0 = rnd(first0[1] * first0[2])
    u1 = rnd(first1[1] * first1[2])
    total = edge(0) + kap * (jnp.exp(-dec * (T - 1)) * u0 + jnp.exp(-dec * (T - 2)) * u1)
    ahead = (me - 1 - slab).astype(F32)
    weight = jnp.exp(-dec * (T * jnp.maximum(ahead, 0.0)))
    carry = jnp.sum(jnp.where(slab < me, weight * total, 0.0), axis=0, keepdims=True)
    carry_next = jnp.exp(-dec * T) * carry + own(total)
    one = jnp.exp(-dec)
    power = jnp.exp(-dec * rows.astype(F32))
    bump = jnp.where(rows >= 1, kap * own(u1) * jnp.exp(dec), 0.0)
    h = h_ref[...] + power * (one * carry + kap * own(u0) + bump)
    q, kf, vf = full
    mix = rnd(h) + skip * rnd(kf * vf)
    gated = (q * mix).astype(BF16)
    gated_ref[...] = gated
    low_ref[...] = dot(gated, down_ref[...]).astype(BF16)
    q_ref[...] = q
    k_ref[...] = kf
    v_ref[...] = vf
    mix_ref[...] = mix
    n0 = following(u0)
    n1 = following(u1)
    h0 = one * carry_next + kap * n0
    h1 = one * h0 + kap * n1
    next_ref[0:1, :] = rnd(h0) + skip * n0
    next_ref[1:2, :] = rnd(h1) + skip * n1
    for i in range(3):
        next_ref[2 + 2 * i : 3 + 2 * i, :] = following(first0[i])
        next_ref[3 + 2 * i : 4 + 2 * i, :] = following(first1[i])


def part_kernel(gated_ref, low_ref, ow_ref, right_ref, left_ref, far_ref, own_ref):
    ids = block_ids()
    gated = gated_ref[...]
    for k, dst in ((3, far_ref), (2, right_ref), (1, left_ref), (0, own_ref)):
        if k > 0:
            dst[1024:1280, :] = low_ref[...]
        for r in range(4):
            cols = pl.ds(pl.multiple_of(ids[k][r] * 256, 256), 256)
            dst[r * 256 : r * 256 + 256, :] = dot(gated, ow_ref[:, cols]).astype(BF16)


def bwd_in_kernel(
    g0, g1, g2, g3, ow_ref, down_ref, q_ref, low_out, cst,
    dg_ref, gsum_ref, edge_ref, last_ref,
):
    rows = row_ids()
    dec = row_of(cst, DEC)
    ids = block_ids()
    pairs = as_pairs((g0, g1, g2, g3), 640)
    dlowd = low_sum(pairs, CUT, 256)
    last = jnp.sum(dlowd * low_out[...].astype(F32), axis=0, keepdims=True)
    last_ref[...] = jnp.broadcast_to(last, (8, RANK))
    dg = dot_nt((dlowd * row_of(cst, PICKED + 3)).astype(BF16), down_ref[...])
    for k, pair in enumerate(pairs):
        for r in range(4):
            cols = pl.ds(pl.multiple_of(ids[k][r] * 256, 256), 256)
            dg = dg + dot_nt(blk(*pair, r, 128), ow_ref[:, cols])
    dg_ref[...] = dg
    g = scan_up(row_of(cst, KAP) * rnd(dg * q_ref[...]), dec, rows)
    gsum_ref[...] = g
    edge_ref[0:2, :] = g[:2]
    edge_ref[2:4, :] = dg[:2]
    edge_ref[4:8, :] = jnp.zeros((4, C), F32)


def bwd_out_kernel(
    near, other, dg_ref, g_ref, q_ref, k_ref, v_ref, mix_ref, next_ref, cst, zraw_ref,
    zlow_ref, low_ref, rstd_ref, last_ref, up_ref, w_ref,
    right_ref, left_ref, far_ref, own_ref, rows_ref, dzb_ref, edges_ref,
):
    me = position()
    ids = block_ids()
    place(edges_ref, near, other)
    rows = row_ids()
    dec = row_of(cst, DEC)
    skip = row_of(cst, SKIP)
    slab = lax.broadcasted_iota(jnp.int32, (SLABS, C), 0)

    def following(v):
        return jnp.sum(jnp.where(slab == me + 1, v, 0.0), axis=0, keepdims=True)

    head = edges_ref[:, 0, :]
    ahead = (slab - me - 1).astype(F32)
    weight = jnp.exp(-dec * (T * jnp.maximum(ahead, 0.0)))
    carry = jnp.sum(jnp.where(slab > me, weight * head, 0.0), axis=0, keepdims=True)
    weight = jnp.exp(-dec * (T * jnp.maximum(ahead - 1.0, 0.0)))
    carry_next = jnp.sum(jnp.where(slab > me + 1, weight * head, 0.0), axis=0, keepdims=True)
    g = g_ref[...] + jnp.exp(-dec * (T - rows).astype(F32)) * carry
    dg = dg_ref[...]
    q, kf, vf = q_ref[...], k_ref[...], v_ref[...]
    dprod = rnd(g) + skip * (dg * q)
    dfeat = (dg * mix_ref[...], dprod * vf, dprod * kf)
    dg0 = following(edges_ref[:, 2, :])
    dg1 = following(edges_ref[:, 3, :])
    g1 = following(edges_ref[:, 1, :]) + jnp.exp(-dec * (T - 1)) * carry_next
    nxt = [row_of(next_ref, n) for n in range(8)]
    dp0 = rnd(carry) + skip * (dg0 * nxt[2])
    dp1 = rnd(g1) + skip * (dg1 * nxt[3])
    inside = jnp.full((1, C), me, jnp.int32) < SLABS - 1
    after0 = [jnp.where(inside, v, 0.0) for v in (dg0 * nxt[0], dp0 * nxt[6], dp0 * nxt[4])]
    after1 = [jnp.where(inside, v, 0.0) for v in (dg1 * nxt[1], dp1 * nxt[7], dp1 * nxt[5])]
    low_raw = low_ref[...]
    low_in = low_raw * rstd_ref[...]
    dlow = jnp.zeros((T, RANK), F32)
    inner = jnp.zeros((T, C), F32)
    grads = []
    for i in range(3):
        t0, t1, t2 = (row_of(cst, TAPS + 3 * i + n) for n in range(3))
        d = dfeat[i]
        s1 = jnp.where(rows == T - 1, after0[i], pltpu.roll(d, T - 1, 0))
        s2 = jnp.where(
            rows == T - 2, after0[i], jnp.where(rows == T - 1, after1[i], pltpu.roll(d, T - 2, 0))
        )
        dz = t0 * d + t1 * s1 + t2 * s2
        dzb_ref[i] = dz.astype(BF16)
        rows_ref[i : i + 1, :] = jnp.sum(dz * zlow_ref[i], axis=0, keepdims=True)
        dlowd = dot_nt((dz * row_of(cst, SCALE + i)).astype(BF16), up_ref[i])
        grads.append(jnp.sum(dlowd * low_in, axis=0, keepdims=True))
        dlow = dlow + dlowd * row_of(cst, PICKED + i)
        inner = inner + dz * zraw_ref[i]
    rows_ref[3:8, :] = jnp.zeros((5, C), F32)
    inner = line(jnp.sum(inner + dlow * low_raw, axis=1, keepdims=True))
    low = dlow.astype(BF16)
    tail = thirds(inner)
    for row in grads + [last_ref[0:1, :]]:
        tail = tail + thirds(row)
    tail = tile_of(tail)
    for k, dst in ((3, far_ref), (2, right_ref), (1, left_ref), (0, own_ref)):
        dst[1024:1280, :] = low
        dst[1280:1296, :] = tail
        for r in range(4):
            at = ids[k][r]
            acc = dot_nt(dzb_ref[0], w_ref[0, at])
            acc = acc + dot_nt(dzb_ref[1], w_ref[1, at])
            acc = acc + dot_nt(dzb_ref[2], w_ref[2, at])
            dst[r * 256 : r * 256 + 256, :] = acc.astype(BF16)


def total_of(parts, lo, hi):
    out = parts[0][lo:hi, :].astype(F32)
    for part in parts[1:]:
        out = out + part[lo:hi, :].astype(F32)
    return out


def out_sum_kernel(
    own, low_ref, rm, lm, fm, c0, c1, c2, c3, whole, cst, near, far, gos_ref,
):
    parts = (own, rm, lm, fm)
    low = low_ref[...].astype(F32) + total_of(parts[1:], 1024, 1280)
    lowd = (low * row_of(cst, PICKED + 3)).astype(BF16)
    gos_ref[4:8, :] = jnp.zeros((4, C), F32)
    for r, z in enumerate((c0, c1, c2, c3)):
        olow = dot(lowd, whole[r * 256 : r * 256 + 256, :])
        scale = joined(z[384:400, :].astype(F32), 0)
        v = total_of(parts, r * 256, r * 256 + 256) + olow * scale
        dst = near if r < 2 else far
        dst[(r % 2) * 256 : (r % 2) * 256 + 256, :] = v.astype(BF16)
        gos_ref[r : r + 1, :] = jnp.sum(z[:256, :].astype(F32) * olow, axis=0, keepdims=True)


def out_half_kernel(near, far, keep, send):
    keep[...] = near[0:256, :].astype(F32) + far[0:256, :].astype(F32)
    send[...] = (near[256:512, :].astype(F32) + far[256:512, :].astype(F32)).astype(BF16)


def in_sum_kernel(
    own, rm, lm, fm, whole, gos, o0, o1, o2, o3, keep,
):
    parts = (own, rm, lm, fm)
    low = total_of(parts, 1024, 1296)
    dlow = low[:256].astype(BF16)
    inner = joined(low[256:], 0)
    grads = [joined(low[256:], 3 + 3 * i) for i in range(4)]
    keep[0:1, :] = inner
    for i in range(4):
        keep[1 + i : 2 + i, :] = grads[i]
    keep[5:6, :] = gos[0:1, :]
    keep[6:8, :] = jnp.zeros((2, C), F32)
    common = []
    for row in [inner] + grads:
        common = common + thirds(row)
    for r, out in enumerate((o0, o1, o2, o3)):
        v = total_of(parts, r * 256, r * 256 + 256)
        v = v + dot_nt(dlow, whole[r * 256 : r * 256 + 256, :])
        out[0:256, :] = v.astype(out.dtype)
        if r > 0:
            out[256:288, :] = tile_of(common + thirds(gos[r : r + 1, :]), 32)


def final_kernel(
    o0, r1, r2, r3, keep, sums, tok, cot, gain, rstd_ref, grad_ref, rows_ref,
):
    dnorm = o0[...]
    rows = [keep[i : i + 1, :] for i in range(6)]
    for ref in (r1, r2, r3):
        dnorm = dnorm + ref[0:256, :].astype(F32)
        tail = ref[256:288, :].astype(F32)
        rows = [rows[i] + joined(tail, 3 * i) for i in range(6)]
    rstd = rstd_ref[...]
    inner = column(rows[0]) * (rstd * rstd * rstd / WIDTH)
    x = tok[...].astype(F32)
    grad = cot[...].astype(F32) + rstd * (gain[...].astype(F32) * dnorm) - x * inner
    grad_ref[...] = grad.astype(BF16)
    rows_ref[0:3, :] = sums[0:3, :]
    rows_ref[3:4, :] = rows[5]
    for i in range(4):
        rows_ref[4 + i : 5 + i, :] = rows[1 + i]


def table_kernel(pick, rep, table_ref, gis_ref, gos_ref):
    rows = rep[0]
    for i in range(1, SLABS):
        rows = rows + rep[i]
    gis_ref[...] = rows[0:3]
    gos_ref[...] = rows[3:4]
    for g in range(4):
        out = jnp.zeros((1, RANK), F32)
        for i in range(4):
            chosen = jnp.full((1, RANK), pick[i], jnp.int32) == g
            out = out + jnp.where(chosen, rows[4 + i : 5 + i], 0.0)
        table_ref[g : g + 1, :] = out


VMEM = pl.BlockSpec(memory_space=pltpu.VMEM)
SMEM = pl.BlockSpec(memory_space=pltpu.SMEM)


def call(kernel, outs, args, scalars=False, scratch=(), flops=1 << 24, after=(), hold=()):
    specs = [VMEM] * len(args)
    if scalars:
        specs[0] = SMEM
    body = kernel
    if after or hold:
        n, m = len(args), len(after) + len(hold)

        def body(*refs):
            kernel(*refs[:n], *refs[n + m :])

        specs = specs + [VMEM] * len(hold) + [pl.BlockSpec(memory_space=pl.ANY)] * len(after)
        args = list(args) + list(hold) + list(after)
    outs = [jax.ShapeDtypeStruct(s, d) for s, d in outs]
    size = sum(v.size * v.dtype.itemsize for v in list(args) + outs)
    return pl.pallas_call(
        body,
        out_shape=outs,
        in_specs=specs,
        out_specs=[VMEM] * len(outs),
        scratch_shapes=list(scratch),
        compiler_params=pltpu.CompilerParams(vmem_limit_bytes=16 * 2**20),
        cost_estimate=pl.CostEstimate(flops=flops, bytes_accessed=size, transcendentals=0),
    )(*args)


def on_device(
    tokens,
    cotangent,
    norm_gain,
    in_weight,
    in_down,
    in_up,
    in_scale,
    scale_table,
    table_pick,
    short_taps,
    residue,
    decay,
    skip_gain,
    out_weight,
    out_down,
    out_up,
    out_scale,
):
    kap = residue * jnp.sqrt(-jnp.expm1(-2.0 * decay))
    weight = jnp.transpose(in_weight, (1, 0, 2)).reshape(3, 16, 256, C)
    up_in = jnp.transpose(in_up, (1, 0, 2))
    gain = norm_gain[None]
    (cst,) = call(
        const_kernel,
        [((24, C), F32)],
        [table_pick, kap[None], decay[None], skip_gain[None], in_scale, short_taps, scale_table],
        scalars=True,
        hold=[weight, up_in],
    )
    half = jnp.where(lax.axis_index("core") == 0, in_down[:128], in_down[128:])
    tz0 = jnp.concatenate([tokens, half, gain, jnp.zeros((15, C), BF16)], 0)
    tz = [tz0] + [across(tz0, "zh", r) for r in (1, 2, 3)]
    (cz0,) = call(
        cot_start_kernel, [((400, C), BF16)], [cotangent, out_up, out_scale[None], tz[2]]
    )
    cz = [cz0] + [across(cz0, "zh", r) for r in (1, 2, 3)]
    (other,) = call(halves_kernel, [((384, C), BF16)], tz[1:], after=[cst])
    pay, dn_all = call(
        token_kernel, [((1296, C), BF16), ((1024, C), BF16)],
        [*tz, swap(other, "core"), in_down],
    )
    tr, near_half = ring_gather(pay, 656)
    (other,) = call(halves_kernel, [((384, C), BF16)], cz[1:], after=[near_half])
    cpay, up_all = call(
        cot_kernel, [((1280, C), BF16), ((1024, C), BF16)], [*cz, swap(other, "core"), out_up],
        after=tr[3:],
    )
    cr = x_gather(cpay)
    zraw, z, zlow, h, edge, low_raw, rstd = call(
        fwd_in_kernel,
        [((3, T, C), F32), ((3, T, C), BF16), ((3, T, C), F32), ((T, C), F32), ((16, C), F32),
         ((T, RANK), F32), ((T, 1), F32)],
        [*tr, weight, up_in, cst],
        after=[cpay],
        flops=2 * T * WIDTH * 3 * C,
    )
    edges, _ = ctx_gather(edge)
    gated, low_out, q, kf, vf, mix, nxt = call(
        fwd_out_kernel,
        [((T, C), BF16)] * 2 + [((T, C), F32)] * 4 + [((8, C), F32)],
        [*edges, z, h, cst, out_down],
        scratch=[pltpu.VMEM((SLABS, 16, C), F32)],
    )
    *out, own_out = call(
        part_kernel,
        [((1280, C), BF16)] * 3 + [((1024, C), BF16)],
        [gated, low_out, out_weight],
        flops=2 * T * WIDTH * C,
    )
    got_out = x_scatter(*out)
    dg, gsum, gedge, last = call(
        bwd_in_kernel,
        [((T, C), F32), ((T, C), F32), ((8, C), F32), ((8, RANK), F32)],
        [*cr, out_weight, out_down, q, low_out, cst],
        after=[own_out],
        flops=2 * T * WIDTH * C,
    )
    gedges, _ = ctx_gather(gedge)
    *out, own, sums = call(
        bwd_out_kernel,
        [((1296, C), BF16)] * 4 + [((8, C), F32)],
        [*gedges, dg, gsum, q, kf, vf, mix, nxt, cst, zraw, zlow, low_raw, rstd, last, up_in,
         weight],
        scratch=[pltpu.VMEM((3, T, C), BF16), pltpu.VMEM((SLABS, 8, C), F32)],
        flops=2 * T * WIDTH * 3 * C,
    )
    got = x_scatter(*out)
    half = [((512, C), BF16)] * 2
    near, far_out, gos = call(
        out_sum_kernel, half + [((8, C), F32)], [own_out, low_out, *got_out, *cz, up_all, cst], after=[sums]
    )
    keep, send = call(
        out_half_kernel, [((T, C), F32), ((T, C), BF16)], [near, across(far_out, "zh", 2)]
    )
    mixed = tokens.astype(F32) + keep + across(send, "zh", 1).astype(F32)
    mixed = mixed.astype(BF16)

    payload = [((T, C), F32)] + [((288, C), BF16)] * 3 + [((8, C), F32)]
    o0, o1, o2, o3, inner = call(
        in_sum_kernel, payload, [own, *got, dn_all, gos], after=[mixed]
    )
    got = [across(o, "zh", r) for r, o in ((1, o1), (2, o2), (3, o3))]
    grad_tokens, rows = call(
        final_kernel,
        [((T, C), BF16), ((8, C), F32)],
        [o0, *got, inner, sums, tokens, cotangent, gain, rstd],
    )
    grad_table, grad_in_scale, grad_out_scale = call(
        table_kernel,
        [((4, RANK), F32), ((3, C), F32), ((1, C), F32)],
        [table_pick, ctx_spread(rows)],
        scalars=True,
    )
    return (mixed, grad_tokens, grad_table, grad_in_scale, grad_out_scale[0])


def solution(mesh):
    fine = Mesh(mesh.devices.reshape(2, 4, 2, 4, 4), CTX + TP)
    return jax.shard_map(
        on_device,
        mesh=fine,
        in_specs=(
            P(CTX, TP),
            P(CTX, TP),
            P(TP),
            P(None, None, TP),
            P(TP, None),
            P(None, None, TP),
            P(None, TP),
            P(),
            P(),
            P(None, None, TP),
            P(TP),
            P(TP),
            P(TP),
            P(TP, None),
            P(TP, None),
            P(None, TP),
            P(TP),
        ),
        out_specs=(P(CTX, TP), P(CTX, TP), P(), P(None, TP), P(TP)),
        check_vma=False,
    )
```

```python
import jax
import jax.numpy as jnp
from jax import lax
from jax.experimental import pallas as pl
from jax.experimental.pallas import tpu as pltpu
from jax.sharding import Mesh, PartitionSpec as P

HIGH = lax.Precision.HIGHEST
CTX = ("zl", "y", "core")
TP = ("x", "zh")
F32 = jnp.float32
BF16 = jnp.bfloat16
T = 256
C = 256
RANK = 256
SLABS = 16
LOW_T = 272
CUT_T = 144
CUT = 128
WIDTH = 4096
KAP, DEC, SKIP, SCALE, TAPS, PICKED = 0, 1, 2, 3, 6, 15


def shift(v, axis, k):
    return lax.ppermute(v, axis, [(i, (i + k) % 4) for i in range(4)])


def swap(v, axis):
    return lax.ppermute(v, axis, [(0, 1), (1, 0)])


def stack(*parts):
    def kernel(*refs):
        for i, ref in enumerate(refs[:-1]):
            refs[-1][i] = ref[...]

    return call(kernel, [((len(parts),) + parts[0].shape, parts[0].dtype)], parts)[0]


def ctx_gather(v):
    first = stack(v, swap(v, "core"))
    v = stack(first, across(first, "y", 1))
    v = stack(v, across(v, "y", 2))
    return [v, swap(v, "zl")], first


def across(v, axis, bit):
    return lax.ppermute(v, axis, [(i, i ^ bit) for i in range(4)])


def ctx_spread(v):
    wide = jnp.broadcast_to(v[None], (SLABS,) + v.shape)
    return lax.all_to_all(wide, CTX, split_axis=0, concat_axis=0, tiled=True)


def place(scr, near, other):
    zl, y, core = (lax.axis_index(a) for a in CTX)
    for kz, src in enumerate((near, other)):
        for ky in range(4):
            for kc in range(2):
                slab = (1 - zl if kz else zl) * 8 + jnp.bitwise_xor(y, ky) * 2
                slab = slab + (1 - core if kc else core)
                scr[slab] = src[ky // 2, ky % 2, kc]


def position():
    zl, y, core = (lax.axis_index(a) for a in CTX)
    return zl * 8 + y * 2 + core


def block_ids():
    x, zh = lax.axis_index("x"), lax.axis_index("zh")
    xs = [x, lax.rem(x + 3, 4), lax.rem(x + 1, 4), lax.rem(x + 2, 4)]
    zs = [jnp.bitwise_xor(zh, r) for r in range(4)]
    return [[a * 4 + b for b in zs] for a in xs]


def x_gather(own):
    return [own, shift(own, "x", 1), shift(own, "x", -1), shift(own, "x", 2)]


def ring_gather(own, cut):
    left, right = shift(own, "x", 1), shift(own, "x", -1)
    rows = own.shape[0]

    def kernel(left_ref, right_ref, fa, fb):
        fa[...] = left_ref[0:cut, :]
        fb[...] = right_ref[cut:rows, :]

    shapes = [((cut, C), BF16), ((rows - cut, C), BF16)]
    fa, fb = call(kernel, shapes, [left, right])
    return [own, left, right, shift(fa, "x", 1), shift(fb, "x", -1)], fa


def x_scatter(right, left, far):
    return [shift(right, "x", 1), shift(left, "x", -1), shift(far, "x", 2)]


def as_pairs(quad, cut):
    return [(g.at[0:cut, :], g.at[cut:, :]) for g in quad]


def dot(a, b):
    return jnp.dot(a, b, preferred_element_type=F32)


def dot_nt(a, b):
    return lax.dot_general(a, b, (((1,), (1,)), ((), ())), preferred_element_type=F32)


def rnd(v):
    return v.astype(BF16).astype(F32)


def row_ids():
    return lax.broadcasted_iota(jnp.int32, (T, C), 0)


def column(row):
    square = (T, T)
    same = lax.broadcasted_iota(jnp.int32, square, 0) == lax.broadcasted_iota(jnp.int32, square, 1)
    return jnp.sum(jnp.where(same, row, 0.0), axis=1, keepdims=True)


def line(col):
    square = (T, T)
    same = lax.broadcasted_iota(jnp.int32, square, 0) == lax.broadcasted_iota(jnp.int32, square, 1)
    return jnp.sum(jnp.where(same, col, 0.0), axis=0, keepdims=True)


def thirds(row):
    hi = rnd(row)
    mid = rnd(row - hi)
    return [hi, mid, row - hi - mid]


def tile_of(rows, n=16):
    at = lax.broadcasted_iota(jnp.int32, (n, C), 0)
    out = jnp.zeros((n, C), F32)
    for i, row in enumerate(rows):
        out = jnp.where(at == i, row, out)
    return out.astype(BF16)


def joined(tile, i):
    return tile[i : i + 1] + tile[i + 1 : i + 2] + tile[i + 2 : i + 3]


def down(v, n, rows):
    return jnp.where(rows >= n, pltpu.roll(v, n, 0), 0.0)


def up(v, n, rows):
    return jnp.where(rows < T - n, pltpu.roll(v, T - n, 0), 0.0)


def scan_down(v, dec, rows):
    for k in range(8):
        n = 1 << k
        v = v + jnp.exp(-dec * n) * down(v, n, rows)
    return v


def scan_up(v, dec, rows):
    for k in range(8):
        n = 1 << k
        v = v + jnp.exp(-dec * n) * up(v, n, rows)
    return v


def row_of(ref, n):
    return ref[n : n + 1, :]


def blk(a_ref, b_ref, r, head):
    if r < 2:
        return a_ref[r * 256 : r * 256 + 256, :]
    at = head + (r - 2) * 256
    return b_ref[at : at + 256, :]


def put_blk(a_ref, b_ref, r, head, v):
    if r < 2:
        a_ref[r * 256 : r * 256 + 256, :] = v
    else:
        at = head + (r - 2) * 256
        b_ref[at : at + 256, :] = v


def low_sum(pairs, cut, low):
    out = []
    for part, size in ((0, cut), (1, low - cut)):
        at = 512 if part == 0 else 0
        v = 0.0
        for pair in pairs:
            v = v + pair[part][at : at + size, :].astype(F32)
        out.append(v)
    return jnp.concatenate(out, 0)


def const_kernel(pick, kap, dec, skip, scale, taps, table, cst):
    cst[0:1, :] = kap[...]
    cst[1:2, :] = dec[...]
    cst[2:3, :] = skip[...]
    cst[3:6, :] = scale[...]
    for i in range(3):
        for j in range(3):
            cst[TAPS + 3 * i + j : TAPS + 3 * i + j + 1, :] = taps[i, j : j + 1, :]
    for i in range(4):
        row = jnp.zeros((1, RANK), F32)
        for g in range(4):
            chosen = jnp.full((1, RANK), pick[i], jnp.int32) == g
            row = row + jnp.where(chosen, table[g : g + 1, :], 0.0)
        cst[PICKED + i : PICKED + i + 1, :] = row
    cst[19:24, :] = jnp.zeros((5, C), F32)


def cot_start_kernel(cot, upw, scale, after, pay):
    core = lax.axis_index("core")
    pay[0:256, :] = cot[...]
    pay[256:384, :] = upw[pl.ds(pl.multiple_of(core * 128, 128), 128), :]
    at = lax.broadcasted_iota(jnp.int32, (16, C), 0)
    rows = after[384:400, :].astype(F32)
    for i, row in enumerate(thirds(scale[...])):
        rows = jnp.where(at == i, row, rows)
    pay[384:400, :] = rows.astype(BF16)


def halves_kernel(z1, z2, z3, out):
    for i, z in enumerate((z1, z2, z3)):
        out[i * 128 : i * 128 + 128, :] = z[256:384, :]


def join_halves(zs, other, own, whole):
    core = lax.axis_index("core")
    whole[0:256, :] = own[...]
    for r in (1, 2, 3):
        mine = pl.ds(pl.multiple_of(r * 256 + core * 128, 128), 128)
        rest = pl.ds(pl.multiple_of(r * 256 + 128 - core * 128, 128), 128)
        whole[mine, :] = zs[r][256:384, :]
        whole[rest, :] = other[r * 128 - 128 : r * 128, :]


def token_kernel(z0, z1, z2, z3, other, dn, out, whole):
    a_ref, b_ref = out.at[0:656, :], out.at[656:1296, :]
    zs = (z0, z1, z2, z3)
    join_halves(zs, other, dn, whole)
    low = jnp.zeros((T, RANK), F32)
    squares = jnp.zeros((T, 1), F32)
    for r, z in enumerate(zs):
        x = z[:256, :].astype(F32)
        gain = z[384:400, :].astype(F32)[:1]
        xg = (x * gain).astype(BF16)
        put_blk(a_ref, b_ref, r, 128, xg)
        low = low + dot(xg, whole[r * 256 : r * 256 + 256, :])
        squares = squares + jnp.sum(x * x, axis=1, keepdims=True)
    low = low.astype(BF16)
    a_ref[512:656, :] = low[:144]
    b_ref[0:112, :] = low[144:]
    b_ref[112:128, :] = tile_of(thirds(line(squares)))


def cot_kernel(z0, z1, z2, z3, other, upw, out, whole):
    a_ref, b_ref = out.at[0:640, :], out.at[640:1280, :]
    zs = (z0, z1, z2, z3)
    join_halves(zs, other, upw, whole)
    low = jnp.zeros((T, RANK), F32)
    for r, z in enumerate(zs):
        cot = z[:256, :]
        scale = joined(z[384:400, :].astype(F32), 0)
        put_blk(a_ref, b_ref, r, 128, cot)
        low = low + dot_nt(
            (cot.astype(F32) * scale).astype(BF16), whole[r * 256 : r * 256 + 256, :]
        )
    low = low.astype(BF16)
    a_ref[512:640, :] = low[:128]
    b_ref[0:128, :] = low[128:]


def fwd_in_kernel(
    g0, g1, g2, ga, gb, w_ref, up_ref, cst,
    zraw_ref, z_ref, zlow_ref, h_ref, edge_ref, low_ref, rstd_ref,
):
    rows = row_ids()
    ids = block_ids()
    pairs = as_pairs((g0, g1, g2), 656) + [(ga, gb)]
    total = low_sum(pairs, CUT_T, LOW_T)
    rstd = column(lax.rsqrt(joined(total[256:], 0) / WIDTH + 1e-06))
    rstd_ref[...] = rstd
    low_ref[...] = total[:256]
    low_in = low_ref[...] * rstd
    dec = row_of(cst, DEC)
    feat = []
    for i in range(3):
        acc = jnp.zeros((T, C), F32)
        for k, pair in enumerate(pairs):
            for r in range(4):
                acc = acc + dot(blk(*pair, r, 128), w_ref[i, ids[k][r]])
        zraw_ref[i] = acc
        zlow = dot((low_in * row_of(cst, PICKED + i)).astype(BF16), up_ref[i])
        zlow_ref[i] = zlow
        z = (acc * rstd + zlow * row_of(cst, SCALE + i)).astype(BF16)
        z_ref[i] = z
        z = z.astype(F32)
        edge_ref[1 + 4 * i : 3 + 4 * i, :] = z[:2]
        edge_ref[3 + 4 * i : 5 + 4 * i, :] = z[T - 2 :]
        if i > 0:
            f = row_of(cst, TAPS + 3 * i) * z
            for tap in (1, 2):
                f = f + row_of(cst, TAPS + 3 * i + tap) * down(z, tap, rows)
            feat.append(f)
    u = jnp.where(rows >= 2, rnd(feat[0] * feat[1]), 0.0)
    h = scan_down(row_of(cst, KAP) * u, dec, rows)
    h_ref[...] = h
    edge_ref[0:1, :] = h[T - 1 :]
    edge_ref[13:16, :] = jnp.zeros((3, C), F32)


def fwd_out_kernel(
    near, other, z_ref, h_ref, cst, down_ref,
    gated_ref, low_ref, q_ref, k_ref, v_ref, mix_ref, next_ref, edges_ref,
):
    me = position()
    place(edges_ref, near, other)
    rows = row_ids()
    dec = row_of(cst, DEC)
    kap = row_of(cst, KAP)
    skip = row_of(cst, SKIP)
    slab = lax.broadcasted_iota(jnp.int32, (SLABS, C), 0)

    def edge(r):
        return edges_ref[:, r, :]

    def prev(v):
        return jnp.where(slab >= 1, pltpu.roll(v, 1, 0), 0.0)

    def own(v):
        return jnp.sum(jnp.where(slab == me, v, 0.0), axis=0, keepdims=True)

    def following(v):
        return jnp.sum(jnp.where(slab == me + 1, v, 0.0), axis=0, keepdims=True)

    first0, first1, full = [], [], []
    for i in range(3):
        t0, t1, t2 = (row_of(cst, TAPS + 3 * i + n) for n in range(3))
        a0, a1 = edge(1 + 4 * i), edge(2 + 4 * i)
        b0, b1 = prev(edge(3 + 4 * i)), prev(edge(4 + 4 * i))
        first0.append(t0 * a0 + t1 * b1 + t2 * b0)
        first1.append(t0 * a1 + t1 * a0 + t2 * b1)
        p0, p1 = own(b0), own(b1)
        z = z_ref[i].astype(F32)
        s1 = jnp.where(rows == 0, p1, pltpu.roll(z, 1, 0))
        s2 = jnp.where(rows == 0, p0, jnp.where(rows == 1, p1, pltpu.roll(z, 2, 0)))
        full.append(t0 * z + t1 * s1 + t2 * s2)
    u0 = rnd(first0[1] * first0[2])
    u1 = rnd(first1[1] * first1[2])
    total = edge(0) + kap * (jnp.exp(-dec * (T - 1)) * u0 + jnp.exp(-dec * (T - 2)) * u1)
    ahead = (me - 1 - slab).astype(F32)
    weight = jnp.exp(-dec * (T * jnp.maximum(ahead, 0.0)))
    carry = jnp.sum(jnp.where(slab < me, weight * total, 0.0), axis=0, keepdims=True)
    carry_next = jnp.exp(-dec * T) * carry + own(total)
    one = jnp.exp(-dec)
    power = jnp.exp(-dec * rows.astype(F32))
    bump = jnp.where(rows >= 1, kap * own(u1) * jnp.exp(dec), 0.0)
    h = h_ref[...] + power * (one * carry + kap * own(u0) + bump)
    q, kf, vf = full
    mix = rnd(h) + skip * rnd(kf * vf)
    gated = (q * mix).astype(BF16)
    gated_ref[...] = gated
    low_ref[...] = dot(gated, down_ref[...]).astype(BF16)
    q_ref[...] = q
    k_ref[...] = kf
    v_ref[...] = vf
    mix_ref[...] = mix
    n0 = following(u0)
    n1 = following(u1)
    h0 = one * carry_next + kap * n0
    h1 = one * h0 + kap * n1
    next_ref[0:1, :] = rnd(h0) + skip * n0
    next_ref[1:2, :] = rnd(h1) + skip * n1
    for i in range(3):
        next_ref[2 + 2 * i : 3 + 2 * i, :] = following(first0[i])
        next_ref[3 + 2 * i : 4 + 2 * i, :] = following(first1[i])


def part_kernel(gated_ref, low_ref, ow_ref, right_ref, left_ref, own_ref):
    ids = block_ids()
    gated = gated_ref[...]
    for k, dst in ((2, right_ref), (1, left_ref), (0, own_ref)):
        if k > 0:
            dst[1024:1280, :] = low_ref[...]
        for r in range(4):
            cols = pl.ds(pl.multiple_of(ids[k][r] * 256, 256), 256)
            dst[r * 256 : r * 256 + 256, :] = dot(gated, ow_ref[:, cols]).astype(BF16)


def far_part_kernel(gated_ref, low_ref, ow_ref, far_ref):
    ids = block_ids()
    gated = gated_ref[...]
    far_ref[1024:1280, :] = low_ref[...]
    for r in range(4):
        cols = pl.ds(pl.multiple_of(ids[3][r] * 256, 256), 256)
        far_ref[r * 256 : r * 256 + 256, :] = dot(gated, ow_ref[:, cols]).astype(BF16)


def bwd_in_kernel(
    g0, g1, g2, g3, ow_ref, down_ref, q_ref, low_out, cst,
    dg_ref, gsum_ref, edge_ref, last_ref,
):
    rows = row_ids()
    dec = row_of(cst, DEC)
    ids = block_ids()
    pairs = as_pairs((g0, g1, g2, g3), 640)
    dlowd = low_sum(pairs, CUT, 256)
    last = jnp.sum(dlowd * low_out[...].astype(F32), axis=0, keepdims=True)
    last_ref[...] = jnp.broadcast_to(last, (8, RANK))
    dg = dot_nt((dlowd * row_of(cst, PICKED + 3)).astype(BF16), down_ref[...])
    for k, pair in enumerate(pairs):
        for r in range(4):
            cols = pl.ds(pl.multiple_of(ids[k][r] * 256, 256), 256)
            dg = dg + dot_nt(blk(*pair, r, 128), ow_ref[:, cols])
    dg_ref[...] = dg
    g = scan_up(row_of(cst, KAP) * rnd(dg * q_ref[...]), dec, rows)
    gsum_ref[...] = g
    edge_ref[0:2, :] = g[:2]
    edge_ref[2:4, :] = dg[:2]
    edge_ref[4:8, :] = jnp.zeros((4, C), F32)


def bwd_out_kernel(
    near, other, dg_ref, g_ref, q_ref, k_ref, v_ref, mix_ref, next_ref, cst, zraw_ref,
    zlow_ref, low_ref, rstd_ref, last_ref, up_ref, w_ref,
    right_ref, left_ref, far_ref, own_ref, rows_ref, dzb_ref, edges_ref,
):
    me = position()
    ids = block_ids()
    place(edges_ref, near, other)
    rows = row_ids()
    dec = row_of(cst, DEC)
    skip = row_of(cst, SKIP)
    slab = lax.broadcasted_iota(jnp.int32, (SLABS, C), 0)

    def following(v):
        return jnp.sum(jnp.where(slab == me + 1, v, 0.0), axis=0, keepdims=True)

    head = edges_ref[:, 0, :]
    ahead = (slab - me - 1).astype(F32)
    weight = jnp.exp(-dec * (T * jnp.maximum(ahead, 0.0)))
    carry = jnp.sum(jnp.where(slab > me, weight * head, 0.0), axis=0, keepdims=True)
    weight = jnp.exp(-dec * (T * jnp.maximum(ahead - 1.0, 0.0)))
    carry_next = jnp.sum(jnp.where(slab > me + 1, weight * head, 0.0), axis=0, keepdims=True)
    g = g_ref[...] + jnp.exp(-dec * (T - rows).astype(F32)) * carry
    dg = dg_ref[...]
    q, kf, vf = q_ref[...], k_ref[...], v_ref[...]
    dprod = rnd(g) + skip * (dg * q)
    dfeat = (dg * mix_ref[...], dprod * vf, dprod * kf)
    dg0 = following(edges_ref[:, 2, :])
    dg1 = following(edges_ref[:, 3, :])
    g1 = following(edges_ref[:, 1, :]) + jnp.exp(-dec * (T - 1)) * carry_next
    nxt = [row_of(next_ref, n) for n in range(8)]
    dp0 = rnd(carry) + skip * (dg0 * nxt[2])
    dp1 = rnd(g1) + skip * (dg1 * nxt[3])
    inside = jnp.full((1, C), me, jnp.int32) < SLABS - 1
    after0 = [jnp.where(inside, v, 0.0) for v in (dg0 * nxt[0], dp0 * nxt[6], dp0 * nxt[4])]
    after1 = [jnp.where(inside, v, 0.0) for v in (dg1 * nxt[1], dp1 * nxt[7], dp1 * nxt[5])]
    low_raw = low_ref[...]
    low_in = low_raw * rstd_ref[...]
    dlow = jnp.zeros((T, RANK), F32)
    inner = jnp.zeros((T, C), F32)
    grads = []
    for i in range(3):
        t0, t1, t2 = (row_of(cst, TAPS + 3 * i + n) for n in range(3))
        d = dfeat[i]
        s1 = jnp.where(rows == T - 1, after0[i], pltpu.roll(d, T - 1, 0))
        s2 = jnp.where(
            rows == T - 2, after0[i], jnp.where(rows == T - 1, after1[i], pltpu.roll(d, T - 2, 0))
        )
        dz = t0 * d + t1 * s1 + t2 * s2
        dzb_ref[i] = dz.astype(BF16)
        rows_ref[i : i + 1, :] = jnp.sum(dz * zlow_ref[i], axis=0, keepdims=True)
        dlowd = dot_nt((dz * row_of(cst, SCALE + i)).astype(BF16), up_ref[i])
        grads.append(jnp.sum(dlowd * low_in, axis=0, keepdims=True))
        dlow = dlow + dlowd * row_of(cst, PICKED + i)
        inner = inner + dz * zraw_ref[i]
    rows_ref[3:8, :] = jnp.zeros((5, C), F32)
    inner = line(jnp.sum(inner + dlow * low_raw, axis=1, keepdims=True))
    low = dlow.astype(BF16)
    tail = thirds(inner)
    for row in grads + [last_ref[0:1, :]]:
        tail = tail + thirds(row)
    tail = tile_of(tail)
    for k, dst in ((3, far_ref), (2, right_ref), (1, left_ref), (0, own_ref)):
        dst[1024:1280, :] = low
        dst[1280:1296, :] = tail
        for r in range(4):
            at = ids[k][r]
            acc = dot_nt(dzb_ref[0], w_ref[0, at])
            acc = acc + dot_nt(dzb_ref[1], w_ref[1, at])
            acc = acc + dot_nt(dzb_ref[2], w_ref[2, at])
            dst[r * 256 : r * 256 + 256, :] = acc.astype(BF16)


def total_of(parts, lo, hi):
    out = parts[0][lo:hi, :].astype(F32)
    for part in parts[1:]:
        out = out + part[lo:hi, :].astype(F32)
    return out


def out_sum_kernel(
    own, low_ref, rm, lm, fm, c0, c1, c2, c3, whole, cst, near, far, gos_ref,
):
    parts = (own, rm, lm, fm)
    low = low_ref[...].astype(F32) + total_of(parts[1:], 1024, 1280)
    lowd = (low * row_of(cst, PICKED + 3)).astype(BF16)
    gos_ref[4:8, :] = jnp.zeros((4, C), F32)
    for r, z in enumerate((c0, c1, c2, c3)):
        olow = dot(lowd, whole[r * 256 : r * 256 + 256, :])
        scale = joined(z[384:400, :].astype(F32), 0)
        v = total_of(parts, r * 256, r * 256 + 256) + olow * scale
        dst = near if r < 2 else far
        dst[(r % 2) * 256 : (r % 2) * 256 + 256, :] = v.astype(BF16)
        gos_ref[r : r + 1, :] = jnp.sum(z[:256, :].astype(F32) * olow, axis=0, keepdims=True)


def out_half_kernel(near, far, keep, send):
    keep[...] = near[0:256, :].astype(F32) + far[0:256, :].astype(F32)
    send[...] = (near[256:512, :].astype(F32) + far[256:512, :].astype(F32)).astype(BF16)


def in_sum_kernel(
    own, rm, lm, fm, whole, gos, o0, o1, o2, o3, keep,
):
    parts = (own, rm, lm, fm)
    low = total_of(parts, 1024, 1296)
    dlow = low[:256].astype(BF16)
    inner = joined(low[256:], 0)
    grads = [joined(low[256:], 3 + 3 * i) for i in range(4)]
    keep[0:1, :] = inner
    for i in range(4):
        keep[1 + i : 2 + i, :] = grads[i]
    keep[5:6, :] = gos[0:1, :]
    keep[6:8, :] = jnp.zeros((2, C), F32)
    common = []
    for row in [inner] + grads:
        common = common + thirds(row)
    for r, out in enumerate((o0, o1, o2, o3)):
        v = total_of(parts, r * 256, r * 256 + 256)
        v = v + dot_nt(dlow, whole[r * 256 : r * 256 + 256, :])
        out[0:256, :] = v.astype(out.dtype)
        if r > 0:
            out[256:288, :] = tile_of(common + thirds(gos[r : r + 1, :]), 32)


def final_kernel(
    o0, r1, r2, r3, keep, sums, tok, cot, gain, rstd_ref, grad_ref, rows_ref,
):
    dnorm = o0[...]
    rows = [keep[i : i + 1, :] for i in range(6)]
    for ref in (r1, r2, r3):
        dnorm = dnorm + ref[0:256, :].astype(F32)
        tail = ref[256:288, :].astype(F32)
        rows = [rows[i] + joined(tail, 3 * i) for i in range(6)]
    rstd = rstd_ref[...]
    inner = column(rows[0]) * (rstd * rstd * rstd / WIDTH)
    x = tok[...].astype(F32)
    grad = cot[...].astype(F32) + rstd * (gain[...].astype(F32) * dnorm) - x * inner
    grad_ref[...] = grad.astype(BF16)
    rows_ref[0:3, :] = sums[0:3, :]
    rows_ref[3:4, :] = rows[5]
    for i in range(4):
        rows_ref[4 + i : 5 + i, :] = rows[1 + i]


def table_kernel(pick, rep, table_ref, gis_ref, gos_ref):
    rows = rep[0]
    for i in range(1, SLABS):
        rows = rows + rep[i]
    gis_ref[...] = rows[0:3]
    gos_ref[...] = rows[3:4]
    for g in range(4):
        out = jnp.zeros((1, RANK), F32)
        for i in range(4):
            chosen = jnp.full((1, RANK), pick[i], jnp.int32) == g
            out = out + jnp.where(chosen, rows[4 + i : 5 + i], 0.0)
        table_ref[g : g + 1, :] = out


VMEM = pl.BlockSpec(memory_space=pltpu.VMEM)
SMEM = pl.BlockSpec(memory_space=pltpu.SMEM)


def call(kernel, outs, args, scalars=False, scratch=(), flops=1 << 24, after=(), hold=()):
    specs = [VMEM] * len(args)
    if scalars:
        specs[0] = SMEM
    body = kernel
    if after or hold:
        n, m = len(args), len(after) + len(hold)

        def body(*refs):
            kernel(*refs[:n], *refs[n + m :])

        specs = specs + [VMEM] * len(hold) + [pl.BlockSpec(memory_space=pl.ANY)] * len(after)
        args = list(args) + list(hold) + list(after)
    outs = [jax.ShapeDtypeStruct(s, d) for s, d in outs]
    size = sum(v.size * v.dtype.itemsize for v in list(args) + outs)
    return pl.pallas_call(
        body,
        out_shape=outs,
        in_specs=specs,
        out_specs=[VMEM] * len(outs),
        scratch_shapes=list(scratch),
        compiler_params=pltpu.CompilerParams(vmem_limit_bytes=16 * 2**20),
        cost_estimate=pl.CostEstimate(flops=flops, bytes_accessed=size, transcendentals=0),
    )(*args)


def on_device(
    tokens,
    cotangent,
    norm_gain,
    in_weight,
    in_down,
    in_up,
    in_scale,
    scale_table,
    table_pick,
    short_taps,
    residue,
    decay,
    skip_gain,
    out_weight,
    out_down,
    out_up,
    out_scale,
):
    kap = residue * jnp.sqrt(-jnp.expm1(-2.0 * decay))
    weight = jnp.transpose(in_weight, (1, 0, 2)).reshape(3, 16, 256, C)
    up_in = jnp.transpose(in_up, (1, 0, 2))
    gain = norm_gain[None]
    (cst,) = call(
        const_kernel,
        [((24, C), F32)],
        [table_pick, kap[None], decay[None], skip_gain[None], in_scale, short_taps, scale_table],
        scalars=True,
        hold=[weight, up_in],
    )
    half = jnp.where(lax.axis_index("core") == 0, in_down[:128], in_down[128:])
    tz0 = jnp.concatenate([tokens, half, gain, jnp.zeros((15, C), BF16)], 0)
    tz = [tz0] + [across(tz0, "zh", r) for r in (1, 2, 3)]
    (cz0,) = call(
        cot_start_kernel, [((400, C), BF16)], [cotangent, out_up, out_scale[None], tz[2]]
    )
    cz = [cz0] + [across(cz0, "zh", r) for r in (1, 2, 3)]
    (other,) = call(halves_kernel, [((384, C), BF16)], tz[1:], after=[cst])
    pay, dn_all = call(
        token_kernel, [((1296, C), BF16), ((1024, C), BF16)],
        [*tz, swap(other, "core"), in_down],
    )
    tr, near_half = ring_gather(pay, 656)
    (other,) = call(halves_kernel, [((384, C), BF16)], cz[1:], after=[near_half])
    cpay, up_all = call(
        cot_kernel, [((1280, C), BF16), ((1024, C), BF16)], [*cz, swap(other, "core"), out_up],
        after=tr[3:],
    )
    cr = x_gather(cpay)
    zraw, z, zlow, h, edge, low_raw, rstd = call(
        fwd_in_kernel,
        [((3, T, C), F32), ((3, T, C), BF16), ((3, T, C), F32), ((T, C), F32), ((16, C), F32),
         ((T, RANK), F32), ((T, 1), F32)],
        [*tr, weight, up_in, cst],
        after=[cpay],
        flops=2 * T * WIDTH * 3 * C,
    )
    edges, _ = ctx_gather(edge)
    gated, low_out, q, kf, vf, mix, nxt = call(
        fwd_out_kernel,
        [((T, C), BF16)] * 2 + [((T, C), F32)] * 4 + [((8, C), F32)],
        [*edges, z, h, cst, out_down],
        scratch=[pltpu.VMEM((SLABS, 16, C), F32)],
    )
    to_right, to_left, own_out = call(
        part_kernel,
        [((1280, C), BF16)] * 2 + [((1024, C), BF16)],
        [gated, low_out, out_weight],
        flops=2 * T * WIDTH * C,
    )
    dg, gsum, gedge, last = call(
        bwd_in_kernel,
        [((T, C), F32), ((T, C), F32), ((8, C), F32), ((8, RANK), F32)],
        [*cr, out_weight, out_down, q, low_out, cst],
        after=[own_out],
        flops=2 * T * WIDTH * C,
    )
    (to_far,) = call(
        far_part_kernel, [((1280, C), BF16)], [gated, low_out, out_weight], after=[dg]
    )
    got_out = x_scatter(to_right, to_left, to_far)
    gedges, _ = ctx_gather(gedge)
    *out, own, sums = call(
        bwd_out_kernel,
        [((1296, C), BF16)] * 4 + [((8, C), F32)],
        [*gedges, dg, gsum, q, kf, vf, mix, nxt, cst, zraw, zlow, low_raw, rstd, last, up_in,
         weight],
        scratch=[pltpu.VMEM((3, T, C), BF16), pltpu.VMEM((SLABS, 8, C), F32)],
        flops=2 * T * WIDTH * 3 * C,
    )
    got = x_scatter(*out)
    half = [((512, C), BF16)] * 2
    near, far_out, gos = call(
        out_sum_kernel, half + [((8, C), F32)], [own_out, low_out, *got_out, *cz, up_all, cst], after=[sums]
    )
    keep, send = call(
        out_half_kernel, [((T, C), F32), ((T, C), BF16)], [near, across(far_out, "zh", 2)]
    )
    mixed = tokens.astype(F32) + keep + across(send, "zh", 1).astype(F32)
    mixed = mixed.astype(BF16)

    payload = [((T, C), F32)] + [((288, C), BF16)] * 3 + [((8, C), F32)]
    o0, o1, o2, o3, inner = call(
        in_sum_kernel, payload, [own, *got, dn_all, gos], after=[mixed]
    )
    got = [across(o, "zh", r) for r, o in ((1, o1), (2, o2), (3, o3))]
    grad_tokens, rows = call(
        final_kernel,
        [((T, C), BF16), ((8, C), F32)],
        [o0, *got, inner, sums, tokens, cotangent, gain, rstd],
    )
    grad_table, grad_in_scale, grad_out_scale = call(
        table_kernel,
        [((4, RANK), F32), ((3, C), F32), ((1, C), F32)],
        [table_pick, ctx_spread(rows)],
        scalars=True,
    )
    return (mixed, grad_tokens, grad_table, grad_in_scale, grad_out_scale[0])


def solution(mesh):
    fine = Mesh(mesh.devices.reshape(2, 4, 2, 4, 4), CTX + TP)
    return jax.shard_map(
        on_device,
        mesh=fine,
        in_specs=(
            P(CTX, TP),
            P(CTX, TP),
            P(TP),
            P(None, None, TP),
            P(TP, None),
            P(None, None, TP),
            P(None, TP),
            P(),
            P(),
            P(None, None, TP),
            P(TP),
            P(TP),
            P(TP),
            P(TP, None),
            P(TP, None),
            P(None, TP),
            P(TP),
        ),
        out_specs=(P(CTX, TP), P(CTX, TP), P(), P(None, TP), P(TP)),
        check_vma=False,
    )
```
